32 devices in a mesh: dp: 8 (over y, x, core), seq: 4 (over z).
Axes of the slice: x: 2, y: 2, z: 4, core: 2. Of those that a mesh axis runs over, the one named last changes fastest.
Arguments:
- tokens: bfloat16 [96, 320, 768], P('dp', 'seq'), may hold values from -6 to 6
- lengths: int32 [96], P('dp'), may hold values from 197 to 577, as said below
- grad_out: bfloat16 [96, 320, 768], P('dp', 'seq'), may hold values from -6 to 6
- query_weight: bfloat16 [768, 768], replicated, may hold values from -0.4375 to 0.4375
- query_bias: bfloat16 [768], replicated, may hold values from -1.796875 to 1.796875
- key_weight: bfloat16 [768, 768], replicated, may hold values from -0.21875 to 0.21875
- value_weight: bfloat16 [768, 768], replicated, may hold values from -0.21875 to 0.21875
- value_bias: bfloat16 [768], replicated, may hold values from -1.796875 to 1.796875
- output_weight: bfloat16 [768, 768], replicated, may hold values from -0.875 to 0.875
- output_bias: bfloat16 [768], replicated, may hold values from -1.796875 to 1.796875
- up_weight: bfloat16 [768, 3072], replicated, may hold values from -0.21875 to 0.21875
- up_bias: bfloat16 [3072], replicated, may hold values from -1.796875 to 1.796875
- down_weight: bfloat16 [3072, 768], replicated, may hold values from -0.21875 to 0.21875
- down_bias: bfloat16 [768], replicated, may hold values from -1.796875 to 1.796875
- first_gain: bfloat16 [768], replicated, may hold values from 0.5 to 1.5
- first_shift: bfloat16 [768], replicated, may hold values from -1.796875 to 1.796875
- second_gain: bfloat16 [768], replicated, may hold values from 0.5 to 1.5
- second_shift: bfloat16 [768], replicated, may hold values from -1.796875 to 1.796875
- router_weight: bfloat16 [768], replicated, may hold values from -0.21875 to 0.21875
Outputs:
- mixed: bfloat16 [96, 320, 768], P('dp', 'seq')
- tokens_grad: bfloat16 [96, 320, 768], P('dp', 'seq')
- grad_query_weight: float32 [768, 768], replicated
- grad_query_bias: float32 [768], replicated
- grad_key_weight: float32 [768, 768], replicated
- grad_value_weight: float32 [768, 768], replicated
- grad_value_bias: float32 [768], replicated
- grad_output_weight: float32 [768, 768], replicated
- grad_output_bias: float32 [768], replicated
- grad_up_weight: float32 [768, 3072], replicated
- grad_up_bias: float32 [3072], replicated
- grad_down_weight: float32 [3072, 768], replicated
- grad_down_bias: float32 [768], replicated
- grad_first_gain: float32 [768], replicated
- grad_first_shift: float32 [768], replicated
- grad_second_gain: float32 [768], replicated
- grad_second_shift: float32 [768], replicated
- grad_router_weight: float32 [768], replicated
The draws below stay inside these ranges and needn't reach their ends.
Inputs may be any that keep to these rules, and one draw needn't show every extreme that they name: `lengths`: each length is 197 or 577; each run of 12 images of one dp index holds at least one of length 577.
All inputs are finite; a program needn't handle non-finite values.
Results may differ from the reference program's by a relative error of at most 0.019.
Values may be sent and summed in bfloat16 or wider, within the bound.
No kernel may reach another device: no remote copies, remote signals or barrier semaphores. Data moves between devices by JAX's collectives and lax.ppermute only.
A program may use at most 256 MiB of HBM per device.

```python
import jax
import jax.numpy as jnp
from jax import lax

D = 768
HEADS = 12
HEAD_DIM = 64
FF = 3072
IMG_DP = 12
LONG_LEN = 577
SHORT_LEN = 197
CAP = 320
IMAGES = 96


def draw_lengths(key, part):
    key = jax.random.fold_in(key, 11)
    first_key, second_key = jax.random.split(key)
    picked = jax.random.randint(first_key, (IMAGES,), 0, 2)
    forced = jax.random.randint(second_key, (IMAGES // IMG_DP,), 0, IMG_DP)
    place = jnp.arange(IMAGES) % IMG_DP
    owner = jnp.arange(IMAGES) // IMG_DP
    marked = jnp.where(place == forced[owner], 1, picked)
    return jnp.where(marked == 1, LONG_LEN, SHORT_LEN).astype(jnp.int32)


def shard_levels(rng, shape, cuts, low, top_value):
    level = 1.0
    for axis_at, parts in cuts:
        heights = jax.random.uniform(jax.random.fold_in(jax.random.fold_in(rng, 6), axis_at), (parts,), jnp.float32, low / len(cuts), top_value / len(cuts))
        level = level * jnp.repeat(jnp.exp(heights), shape[axis_at] // parts).reshape((-1,) + (1,) * (len(shape) - 1 - axis_at))
    return level


def gaussian(stream_key, dims, deviation, reach, cuts=(), kind=jnp.bfloat16):
    drawn = jax.random.normal(stream_key, dims, jnp.float32) * deviation
    if len(cuts) > 0:
        drawn = shard_levels(stream_key, dims, cuts, -0.22, 0.18) * drawn
    return jnp.clip(drawn, min=-reach, max=reach).astype(kind)


def setup_inputs(seed: int = 0) -> dict:
    streams_of = jax.random.split(jax.random.key(seed), 20)
    tokens = gaussian(streams_of[0], (IMAGES, CAP, D), 1.0, 6.0, ((0, 8), (1, 4)))
    lengths = draw_lengths(jax.random.fold_in(streams_of[19], 71), 0)
    grad_out = gaussian(streams_of[2], (IMAGES, CAP, D), 1.0, 6.0, ((0, 8), (1, 4)))
    query_weight = gaussian(streams_of[3], (D, D), (D // 4) ** -0.5, 0.4375)
    query_bias = gaussian(streams_of[4], (D,), 0.3, 1.796875)
    key_weight = gaussian(streams_of[5], (D, D), D ** -0.5, 0.21875)
    value_weight = gaussian(streams_of[6], (D, D), D ** -0.5, 0.21875)
    value_bias = gaussian(streams_of[7], (D,), 0.3, 1.796875)
    output_weight = gaussian(streams_of[8], (D, D), (D // 16) ** -0.5, 0.875)
    output_bias = gaussian(streams_of[9], (D,), 0.3, 1.796875)
    up_weight = gaussian(streams_of[10], (D, FF), D ** -0.5, 0.21875)
    up_bias = gaussian(streams_of[11], (FF,), 0.3, 1.796875)
    down_weight = gaussian(streams_of[12], (FF, D), (FF // 4) ** -0.5, 0.21875)
    down_bias = gaussian(streams_of[13], (D,), 0.3, 1.796875)
    first_gain = jnp.clip(1.0 + 0.1 * jax.random.normal(streams_of[14], (D,), jnp.float32), 0.5, 1.5).astype(jnp.bfloat16)
    first_shift = gaussian(streams_of[15], (D,), 0.3, 1.796875)
    second_gain = jnp.clip(1.0 + 0.1 * jax.random.normal(streams_of[16], (D,), jnp.float32), 0.5, 1.5).astype(jnp.bfloat16)
    second_shift = gaussian(streams_of[17], (D,), 0.3, 1.796875)
    router_weight = gaussian(streams_of[18], (D,), D ** -0.5, 0.21875)
    return {"tokens": tokens, "lengths": lengths, "grad_out": grad_out, "query_weight": query_weight, "query_bias": query_bias, "key_weight": key_weight, "value_weight": value_weight, "value_bias": value_bias, "output_weight": output_weight, "output_bias": output_bias, "up_weight": up_weight, "up_bias": up_bias, "down_weight": down_weight, "down_bias": down_bias, "first_gain": first_gain, "first_shift": first_shift, "second_gain": second_gain, "second_shift": second_shift, "router_weight": router_weight}


@jax.custom_vjp
def low(v):
    return lax.optimization_barrier(v.astype(jnp.bfloat16)).astype(jnp.float32)

@jax.custom_vjp
def low_back(v):
    return v

def low_keep(v):
    return (low(v), None)

def low_pass(kept, grad):
    return (grad,)

def back_keep(v):
    return (v, None)

def back_low(kept, grad):
    return (low(grad),)
low.defvjp(low_keep, low_pass)
low_back.defvjp(back_keep, back_low)

def normalize(field, gain, shift):
    middle = lax.optimization_barrier(jnp.mean(field, axis=-1, keepdims=True))
    centred = field - middle
    spread = lax.optimization_barrier(jnp.mean(centred * centred, axis=-1, keepdims=True))
    return centred * lax.rsqrt(spread + 1e-06) * gain + shift

def product(left, right):
    return jnp.matmul(left, right, precision=lax.Precision.HIGHEST)

def forward(field, params, valid):
    query_weight, query_bias, key_weight, value_weight, value_bias, output_weight, output_bias, up_weight, up_bias, down_weight, down_bias, first_gain, first_shift, second_gain, second_shift, router_weight = params
    images = field.shape[0]
    slots = field.shape[1]
    normed = low(normalize(field, first_gain, first_shift))
    gate = jax.nn.sigmoid(jnp.einsum('icd,d->ic', normed, router_weight, precision=lax.Precision.HIGHEST))
    weight_row = valid * gate
    queries = low(low_back(product(normed, query_weight) + query_bias))
    keys = low(low_back(product(normed, key_weight)))
    values = low(low_back(product(normed, value_weight) + value_bias))
    shape = (images, slots, HEADS, HEAD_DIM)
    scores = low_back(jnp.einsum('iqhe,ikhe->ihqk', queries.reshape(shape), keys.reshape(shape), precision=lax.Precision.HIGHEST) * HEAD_DIM ** (-0.5))
    scores = jnp.where(valid[:, None, None, :] > 0, scores, -1e+30)
    top = lax.optimization_barrier(jnp.max(scores, axis=-1, keepdims=True))
    expo = jnp.exp(scores - top)
    probs = low(expo / lax.optimization_barrier(jnp.sum(expo, axis=-1, keepdims=True)))
    context = jnp.einsum('ihqk,ikhe->iqhe', probs, values.reshape(shape), precision=lax.Precision.HIGHEST)
    context = low(low_back(context.reshape(images, slots, D)))
    branch_one = low_back(product(context, output_weight) + output_bias)
    middle = field + weight_row[..., None] * branch_one
    second = low(normalize(middle, second_gain, second_shift))
    hidden = low_back(product(second, up_weight) + up_bias)
    activated = low(jax.nn.gelu(hidden, approximate=False))
    branch_two = low_back(product(activated, down_weight) + down_bias)
    return middle + weight_row[..., None] * branch_two

def reference(tokens, lengths, grad_out, query_weight, query_bias, key_weight, value_weight, value_bias, output_weight, output_bias, up_weight, up_bias, down_weight, down_bias, first_gain, first_shift, second_gain, second_shift, router_weight):
    params = tuple((weight.astype(jnp.float32) for weight in (query_weight, query_bias, key_weight, value_weight, value_bias, output_weight, output_bias, up_weight, up_bias, down_weight, down_bias, first_gain, first_shift, second_gain, second_shift, router_weight)))
    slots = tokens.shape[1]
    counts = (lengths + 1) // 2
    valid = (jnp.arange(slots, dtype=jnp.int32)[None, :] < counts[:, None]).astype(jnp.float32)
    groups = tokens.shape[0] // IMG_DP
    inputs = tokens.astype(jnp.float32).reshape(groups, IMG_DP, slots, D)
    upstream = grad_out.astype(jnp.float32).reshape(groups, IMG_DP, slots, D)
    valid_groups = valid.reshape(groups, IMG_DP, slots)

    def one_group(totals, item):
        field, cotangent, mask = item
        result, pull = jax.vjp(lambda values, weights: forward(values, weights, mask), field, params)
        grad_field, grad_weights = pull(cotangent)
        totals = jax.tree.map(lambda first, other: first + other, totals, grad_weights)
        return (totals, (result, grad_field))
    start = jax.tree.map(jnp.zeros_like, params)
    totals, (results, grad_fields) = lax.scan(one_group, start, (inputs, upstream, valid_groups))
    mixed = results.reshape(tokens.shape).astype(jnp.bfloat16)
    tokens_grad = grad_fields.reshape(tokens.shape).astype(jnp.bfloat16)
    return (mixed, tokens_grad, totals[0], totals[1], totals[2], totals[3], totals[4], totals[5], totals[6], totals[7], totals[8], totals[9], totals[10], totals[11], totals[12], totals[13], totals[14], totals[15])
```

```python
from functools import partial

import jax
import jax.numpy as jnp
from jax import lax
from jax.sharding import PartitionSpec as P

HEADS = 12
HEAD_DIM = 64


EPSILON = 1e-06


def normalize(field, gain, shift):
    middle = jnp.mean(field, axis=-1, keepdims=True)
    centred = field - middle
    spread = jnp.mean(centred * centred, axis=-1, keepdims=True)
    return centred * lax.rsqrt(spread + EPSILON) * gain + shift


def project(left, right):
    return jnp.einsum("icn,no->ico", left, right, preferred_element_type=jnp.float32)


def back_project(grad, weight):
    return jnp.einsum("ico,no->icn", grad, weight, preferred_element_type=jnp.float32)


def outer_sum(left, right):
    return jnp.einsum("icn,ico->no", left, right, preferred_element_type=jnp.float32)


def column_sum(grad):
    return jnp.sum(grad.astype(jnp.float32), axis=(0, 1))


def split_heads(field):
    return field.reshape(field.shape[0], field.shape[1], HEADS, HEAD_DIM)


def scores_of(queries, keys_all, key_valid):
    raw = jnp.einsum(
        "iqhe,ikhe->ihqk",
        split_heads(queries),
        split_heads(keys_all),
        preferred_element_type=jnp.float32,
    ) * HEAD_DIM ** (-0.5)
    return jnp.where(key_valid[:, None, None, :] > 0, raw, -1e30)


def to_images(field):
    return lax.all_to_all(field, "seq", split_axis=0, concat_axis=1, tiled=True)


def to_slots(field):
    return lax.all_to_all(field, "seq", split_axis=1, concat_axis=0, tiled=True)


def sum_devices(grad):
    share = lax.psum_scatter(
        grad.astype(jnp.bfloat16), ("dp", "seq"), scatter_dimension=0, tiled=True
    )
    return lax.all_gather(share, ("dp", "seq"), axis=0, tiled=True).astype(jnp.float32)


def on_device(
    tokens,
    lengths,
    grad_out,
    query_weight,
    query_bias,
    key_weight,
    value_weight,
    value_bias,
    output_weight,
    output_bias,
    up_weight,
    up_bias,
    down_weight,
    down_bias,
    first_gain,
    first_shift,
    second_gain,
    second_shift,
    router_weight,
):
    tokens = to_images(tokens)
    grad_out = to_images(grad_out)
    images, slots, width = tokens.shape
    total_slots = slots
    lengths = lax.dynamic_slice_in_dim(lengths, lax.axis_index("seq") * images, images)
    counts = (lengths + 1) // 2
    valid = (jnp.arange(slots, dtype=jnp.int32)[None, :] < counts[:, None]).astype(jnp.float32)
    key_valid = valid
    router_float = router_weight.astype(jnp.float32)
    inputs = tokens.astype(jnp.float32)
    first_norm, first_pull = jax.vjp(
        normalize, inputs, first_gain.astype(jnp.float32), first_shift.astype(jnp.float32)
    )
    normed = first_norm.astype(jnp.bfloat16)
    gate = jax.nn.sigmoid(
        jnp.einsum("icd,d->ic", normed, router_weight, preferred_element_type=jnp.float32)
    )
    weight_row = valid * gate
    queries = (project(normed, query_weight) + query_bias.astype(jnp.float32)).astype(jnp.bfloat16)
    keys_local = project(normed, key_weight).astype(jnp.bfloat16)
    values_local = (project(normed, value_weight) + value_bias.astype(jnp.float32)).astype(
        jnp.bfloat16
    )
    keys_all, values_all = keys_local, values_local
    scores = scores_of(queries, keys_all, key_valid)
    top = jnp.max(scores, axis=-1, keepdims=True)
    expo = jnp.exp(scores - top)
    total = jnp.sum(expo, axis=-1, keepdims=True)
    log_total = top + jnp.log(total)
    probs_low = (expo / total).astype(jnp.bfloat16)
    context = jnp.einsum(
        "ihqk,ikhe->iqhe", probs_low, split_heads(values_all), preferred_element_type=jnp.float32
    ).reshape(images, slots, width)
    context_low = context.astype(jnp.bfloat16)
    branch_one = project(context_low, output_weight) + output_bias.astype(jnp.float32)
    middle = inputs + weight_row[..., None] * branch_one
    second_norm, second_pull = jax.vjp(
        normalize, middle, second_gain.astype(jnp.float32), second_shift.astype(jnp.float32)
    )
    second_low = second_norm.astype(jnp.bfloat16)
    hidden = project(second_low, up_weight) + up_bias.astype(jnp.float32)
    activated, gelu_pull = jax.vjp(partial(jax.nn.gelu, approximate=False), hidden)
    activated_low = activated.astype(jnp.bfloat16)
    branch_two = project(activated_low, down_weight) + down_bias.astype(jnp.float32)
    mixed = (middle + weight_row[..., None] * branch_two).astype(jnp.bfloat16)
    upstream = grad_out.astype(jnp.float32)
    grad_branch_two = (weight_row[..., None] * upstream).astype(jnp.bfloat16)
    grad_down_bias = column_sum(grad_branch_two)
    grad_down_weight = outer_sum(activated_low, grad_branch_two)
    (grad_hidden,) = gelu_pull(back_project(grad_branch_two, down_weight))
    grad_hidden_low = grad_hidden.astype(jnp.bfloat16)
    grad_up_bias = column_sum(grad_hidden_low)
    grad_up_weight = outer_sum(second_low, grad_hidden_low)
    grad_middle, grad_second_gain, grad_second_shift = second_pull(
        back_project(grad_hidden_low, up_weight)
    )
    grad_middle = grad_middle + upstream
    grad_gate_row = valid * (
        jnp.sum(upstream * branch_two, axis=-1) + jnp.sum(grad_middle * branch_one, axis=-1)
    )
    grad_branch_one = (weight_row[..., None] * grad_middle).astype(jnp.bfloat16)
    grad_output_bias = column_sum(grad_branch_one)
    grad_output_weight = outer_sum(context_low, grad_branch_one)
    grad_context = back_project(grad_branch_one, output_weight).astype(jnp.bfloat16)
    keys_back, values_back = keys_local, values_local
    probs_again = jnp.exp(scores_of(queries, keys_back, key_valid) - log_total)
    grad_probs = jnp.einsum(
        "iqhe,ikhe->ihqk",
        split_heads(grad_context),
        split_heads(values_back),
        preferred_element_type=jnp.float32,
    )
    centre = jnp.sum(probs_again * grad_probs, axis=-1, keepdims=True)
    grad_scores = (probs_again * (grad_probs - centre)).astype(jnp.bfloat16)
    scale = HEAD_DIM ** (-0.5)
    grad_queries = (
        jnp.einsum(
            "ihqk,ikhe->iqhe",
            grad_scores,
            split_heads(keys_back),
            preferred_element_type=jnp.float32,
        )
        * scale
    ).reshape(images, slots, width)
    grad_queries = grad_queries.astype(jnp.bfloat16)
    grad_keys_term = (
        jnp.einsum(
            "ihqk,iqhe->ikhe", grad_scores, split_heads(queries), preferred_element_type=jnp.float32
        )
        * scale
    ).reshape(images, total_slots, width)
    grad_values_term = jnp.einsum(
        "ihqk,iqhe->ikhe",
        probs_again.astype(jnp.bfloat16),
        split_heads(grad_context),
        preferred_element_type=jnp.float32,
    ).reshape(images, total_slots, width)
    grad_keys_low = grad_keys_term.astype(jnp.bfloat16)
    grad_values_low = grad_values_term.astype(jnp.bfloat16)
    grad_query_bias = column_sum(grad_queries)
    grad_value_bias = column_sum(grad_values_low)
    grad_query_weight = outer_sum(normed, grad_queries)
    grad_key_weight = outer_sum(normed, grad_keys_low)
    grad_value_weight = outer_sum(normed, grad_values_low)
    grad_logit = grad_gate_row * gate * (1.0 - gate)
    grad_router_weight = jnp.einsum(
        "icd,ic->d", normed, grad_logit, preferred_element_type=jnp.float32
    )
    grad_normed = (
        back_project(grad_queries, query_weight)
        + back_project(grad_keys_low, key_weight)
        + back_project(grad_values_low, value_weight)
        + grad_logit[..., None] * router_float
    )
    grad_inputs, grad_first_gain, grad_first_shift = first_pull(grad_normed)
    tokens_grad = (grad_inputs + grad_middle).astype(jnp.bfloat16)
    mixed = to_slots(mixed)
    tokens_grad = to_slots(tokens_grad)
    grad_down_weight = sum_devices(grad_down_weight)
    grad_up_weight = sum_devices(grad_up_weight)
    four = sum_devices(
        jnp.concatenate(
            [grad_query_weight, grad_key_weight, grad_value_weight, grad_output_weight]
        )
    ).reshape(4, width, width)
    small = [
        grad_query_bias,
        grad_value_bias,
        grad_output_bias,
        grad_up_bias,
        grad_down_bias,
        grad_first_gain,
        grad_first_shift,
        grad_second_gain,
        grad_second_shift,
        grad_router_weight,
    ]
    small = lax.psum(jnp.concatenate([piece.reshape(-1, width) for piece in small]), ("dp", "seq"))
    ratio = up_bias.shape[0] // width
    return (
        mixed,
        tokens_grad,
        four[0],
        small[0],
        four[1],
        four[2],
        small[1],
        four[3],
        small[2],
        grad_up_weight,
        small[3 : 3 + ratio].reshape(-1),
        grad_down_weight,
        *[small[3 + ratio + i] for i in range(6)],
    )


def solution(mesh):
    in_specs = (
        P("dp", "seq", None),
        P("dp"),
        P("dp", "seq", None),
        P(),
        P(),
        P(),
        P(),
        P(),
        P(),
        P(),
        P(),
        P(),
        P(),
        P(),
        P(),
        P(),
        P(),
        P(),
        P(),
    )
    out_specs = (
        P("dp", "seq", None),
        P("dp", "seq", None),
        P(),
        P(),
        P(),
        P(),
        P(),
        P(),
        P(),
        P(),
        P(),
        P(),
        P(),
        P(),
        P(),
        P(),
        P(),
        P(),
    )
    return jax.shard_map(
        on_device, mesh=mesh, in_specs=in_specs, out_specs=out_specs, check_vma=False
    )
```

```python
import functools
import math

import jax
import jax.numpy as jnp
from jax import lax
from jax.experimental import pallas as pl
from jax.experimental.pallas import tpu as pltpu
from jax.sharding import PartitionSpec as P

HEADS = 12
HEAD_DIM = 64
EPSILON = 1e-06
PAIR = 2 * HEAD_DIM
LANES = 128
SCALE = HEAD_DIM ** (-0.5)
SCORE_FACTOR = SCALE * math.log2(math.e)
ROOT_HALF = math.sqrt(0.5)
DENSITY = 1.0 / math.sqrt(2.0 * math.pi)
MASKED = -1e30
TILE = 256
VMEM = 56 * 1024 * 1024
F32 = jnp.float32
BF16 = jnp.bfloat16

QB, VB, OB, G1, S1, G2, S2, RW, DB = range(9)


def nn(a, b):
    return lax.dot_general(a, b, (((1,), (0,)), ((), ())), preferred_element_type=F32)


def nt(a, b):
    return lax.dot_general(a, b, (((1,), (1,)), ((), ())), preferred_element_type=F32)


def tn(a, b):
    return lax.dot_general(a, b, (((0,), (0,)), ((), ())), preferred_element_type=F32)


def hat(field):
    mean = jnp.mean(field, axis=-1, keepdims=True)
    centred = field - mean
    spread = jnp.mean(centred * centred, axis=-1, keepdims=True)
    scale = lax.rsqrt(spread + EPSILON)
    return centred * scale, scale


def hat_back(grad, normal, scale):
    first = jnp.mean(grad, axis=-1, keepdims=True)
    second = jnp.mean(grad * normal, axis=-1, keepdims=True)
    return scale * (grad - first - normal * second)


def row_sum(field):
    return jnp.sum(field, axis=0, keepdims=True)


def head_masks():
    lane = lax.broadcasted_iota(jnp.int32, (1, PAIR), 1)
    return [
        jnp.where(lane < HEAD_DIM, 1.0, 0.0).astype(BF16),
        jnp.where(lane < HEAD_DIM, 0.0, 1.0).astype(BF16),
    ]


def attention_kernel(
    counts,
    x_ref,
    vec,
    wq,
    wk,
    wv,
    wo,
    normed_ref,
    q_ref,
    k_ref,
    v_ref,
    ctx_ref,
    middle_ref,
    one_ref,
    second_ref,
    gate_ref,
    row_ref,
    lse_ref,
):
    slots = x_ref.shape[1]
    count = counts[pl.program_id(0)]
    x = x_ref[0].astype(F32)
    normal, _ = hat(x)
    normed = (normal * vec[G1 : G1 + 1] + vec[S1 : S1 + 1]).astype(BF16)
    normed_ref[0] = normed
    logit = jnp.sum(normed.astype(F32) * vec[RW : RW + 1], axis=-1, keepdims=True)
    gate = jax.nn.sigmoid(logit)
    inside = lax.broadcasted_iota(jnp.int32, (slots, 1), 0) < count
    row = jnp.where(inside, gate, 0.0)
    gate_ref[0] = jnp.broadcast_to(gate, (slots, LANES))
    row_ref[0] = jnp.broadcast_to(row, (slots, LANES))
    q_ref[0] = (nn(normed, wq[...]) + vec[QB : QB + 1]).astype(BF16)
    k_ref[0] = nn(normed, wk[...]).astype(BF16)
    v_ref[0] = (nn(normed, wv[...]) + vec[VB : VB + 1]).astype(BF16)
    key_mask = jnp.where(
        lax.broadcasted_iota(jnp.int32, (1, slots), 1) < count, 0.0, MASKED
    )
    masks = head_masks()
    lane = lax.broadcasted_iota(jnp.int32, (1, LANES), 1)
    ones = jnp.ones((slots, LANES), BF16)
    lse = jnp.zeros((slots, LANES), F32)
    for pair in range(HEADS // 2):
        at = slice(pair * PAIR, (pair + 1) * PAIR)
        queries = q_ref[0, :, at]
        keys = k_ref[0, :, at]
        values = jnp.concatenate([v_ref[0, :, at], ones], axis=1)
        halves = []
        for e in range(2):
            scores = nt(queries * masks[e], keys) * SCORE_FACTOR + key_mask
            top = jnp.max(scores, axis=-1, keepdims=True)
            expo = jnp.exp2(scores - top).astype(BF16)
            mixed = nn(expo, values)
            total = mixed[:, PAIR:]
            halves.append(mixed[:, :PAIR] / total)
            lse = jnp.where(lane == 2 * pair + e, top + jnp.log2(total), lse)
        low = jnp.where(lane < HEAD_DIM, halves[0], halves[1])
        ctx_ref[0, :, at] = low.astype(BF16)
    lse_ref[0] = lse
    one = nn(ctx_ref[0], wo[...]) + vec[OB : OB + 1]
    one_ref[0] = one
    middle = x + row * one
    middle_ref[0] = middle
    again, _ = hat(middle)
    second_ref[0] = (again * vec[G2 : G2 + 1] + vec[S2 : S2 + 1]).astype(BF16)


def run_attention(counts, tokens, vectors, wq, wk, wv, wo):
    images, slots, width = tokens.shape
    image = lambda *shape: pl.BlockSpec((1, slots) + shape, lambda i, c: (i, 0, 0))
    whole = lambda a: pl.BlockSpec(a.shape, lambda i, c: (0,) * a.ndim)
    like = lambda lanes, dtype: jax.ShapeDtypeStruct((images, slots, lanes), dtype)
    outs = [(width, BF16)] * 5 + [(width, F32)] * 2 + [(width, BF16)] + [(LANES, F32)] * 3
    flops = 2 * images * slots * width * (4 * width + 2 * slots)
    return pl.pallas_call(
        attention_kernel,
        grid_spec=pltpu.PrefetchScalarGridSpec(
            num_scalar_prefetch=1,
            grid=(images,),
            in_specs=[image(width)] + [whole(a) for a in (vectors, wq, wk, wv, wo)],
            out_specs=[image(lanes) for lanes, _ in outs],
        ),
        out_shape=[like(*o) for o in outs],
        compiler_params=pltpu.CompilerParams(vmem_limit_bytes=VMEM),
        cost_estimate=pl.CostEstimate(
            flops=flops, bytes_accessed=40_000_000, transcendentals=images * HEADS * slots * slots
        ),
        name="attention_forward",
    )(counts, tokens, vectors, wq, wk, wv, wo)


def feed_body(second, back, up, bias, down, two, pulled, down_grad, up_grad, bias_grad):
    hidden = nn(second[...], up[...]) + bias[...]
    phi = 0.5 + 0.5 * lax.erf(hidden * ROOT_HALF)
    density = DENSITY * jnp.exp(-0.5 * hidden * hidden)
    active = (hidden * phi).astype(BF16)
    slope = phi + hidden * density
    two[...] += nn(active, down[...])
    grad_hidden = nt(back[...], down[...]) * slope
    low = grad_hidden.astype(BF16)
    bias_grad[...] = row_sum(low.astype(F32))
    pulled[...] += nt(low, up[...])
    down_grad[...] = tn(active, back[...]).astype(BF16)
    up_grad[...] = tn(second[...], low).astype(BF16)


def feed_first_kernel(
    half,
    second,
    grad_out,
    row,
    up,
    bias,
    down,
    back,
    two,
    pulled,
    down_grad,
    up_grad,
    bias_grad,
    back_sum,
):
    @pl.when(pl.program_id(0) == 0)
    def _():
        value = (row[:, :1] * grad_out[...].astype(F32)).astype(BF16)
        back[...] = value
        back_sum[...] = row_sum(value.astype(F32))
        two[...] = jnp.zeros_like(two)
        pulled[...] = jnp.zeros_like(pulled)

    feed_body(second, back, up, bias, down, two, pulled, down_grad, up_grad, bias_grad)


def feed_second_kernel(
    half,
    second,
    grad_out,
    row,
    up,
    bias,
    down,
    back,
    two_in,
    pulled_in,
    middle,
    one,
    gate,
    vec,
    down_grad,
    up_grad,
    bias_grad,
    mixed,
    grad_middle,
    grad_one,
    grad_logit,
    sums,
    two,
    pulled,
    *,
    block,
):
    @pl.when(pl.program_id(0) == 0)
    def _():
        two[...] = two_in[...]
        pulled[...] = pulled_in[...]

    feed_body(second, back, up, bias, down, two, pulled, down_grad, up_grad, bias_grad)

    @pl.when(pl.program_id(0) == pl.num_programs(0) - 1)
    def _():
        width = second.shape[1]
        zero = jnp.zeros((1, width), F32)

        def step(b, carry):
            gain_sum, shift_sum, one_sum = carry
            at = pl.ds(pl.multiple_of(b * block, block), block)
            upstream = grad_out[at, :].astype(F32)
            weight = row[at, :1]
            branch_two = two[at, :] + vec[DB : DB + 1]
            centre = middle[at, :]
            mixed[at, :] = (centre + weight * branch_two).astype(BF16)
            normal, scale = hat(centre)
            grad = pulled[at, :]
            gain_sum = gain_sum + row_sum(grad * normal)
            shift_sum = shift_sum + row_sum(grad)
            total = hat_back(grad * vec[G2 : G2 + 1], normal, scale) + upstream
            grad_middle[at, :] = total
            low = (weight * total).astype(BF16)
            grad_one[at, :] = low
            one_sum = one_sum + row_sum(low.astype(F32))
            gated = jnp.sum(upstream * branch_two + total * one[at, :], axis=-1, keepdims=True)
            grad_logit[at, :] = weight * (1.0 - gate[at, :]) * gated
            return gain_sum, shift_sum, one_sum

        gain_sum, shift_sum, one_sum = lax.fori_loop(
            0, second.shape[0] // block, step, (zero, zero, zero)
        )
        sums[0:1] = gain_sum
        sums[1:2] = shift_sum
        sums[2:3] = one_sum


def run_feed(which, second, grad_out, row, up, bias, down, later=None):
    rows, width = second.shape
    units = up.shape[1] // 2
    tiles = units // TILE
    whole = lambda a: pl.BlockSpec(a.shape, lambda t, h: (0,) * len(a.shape))
    shape = jax.ShapeDtypeStruct
    wide, tall = (
        pl.BlockSpec((width, TILE), lambda t, h: (0, h[0] * tiles + t)),
        pl.BlockSpec((TILE, width), lambda t, h: (h[0] * tiles + t, 0)),
    )
    in_specs = [whole(second), whole(grad_out), whole(row)]
    in_specs += [wide, pl.BlockSpec((1, TILE), lambda t, h: (0, h[0] * tiles + t)), tall]
    tile_outs = [shape((units, width), BF16), shape((width, units), BF16), shape((1, units), F32)]
    tile_specs = [
        pl.BlockSpec((TILE, width), lambda t, h: (t, 0)),
        pl.BlockSpec((width, TILE), lambda t, h: (0, t)),
        pl.BlockSpec((1, TILE), lambda t, h: (0, t)),
    ]
    field = lambda dtype: shape((rows, width), dtype)
    args = [second, grad_out, row, up, bias, down]
    scratch = []
    if later is None:
        body = feed_first_kernel
        outs = [field(BF16), field(F32), field(F32)] + tile_outs + [shape((1, width), F32)]
        specs = [whole(o) for o in outs[:3]] + tile_specs + [whole(outs[-1])]
    else:
        body = functools.partial(feed_second_kernel, block=math.gcd(rows, 80))
        args += later
        in_specs += [whole(a) for a in later]
        more = [field(BF16), field(F32), field(BF16), shape(row.shape, F32), shape((8, width), F32)]
        outs = tile_outs + more
        specs = tile_specs + [whole(o) for o in more]
        scratch = [pltpu.VMEM((rows, width), F32)] * 2
    return pl.pallas_call(
        body,
        grid_spec=pltpu.PrefetchScalarGridSpec(
            num_scalar_prefetch=1,
            grid=(tiles,),
            in_specs=in_specs,
            out_specs=specs,
            scratch_shapes=scratch,
        ),
        out_shape=outs,
        compiler_params=pltpu.CompilerParams(vmem_limit_bytes=VMEM),
        cost_estimate=pl.CostEstimate(
            flops=12 * rows * width * units, bytes_accessed=30_000_000, transcendentals=2 * rows * units
        ),
        name="feed_first" if later is None else "feed_second",
    )(which, *args)


def attention_back_kernel(
    counts,
    x_ref,
    q_ref,
    k_ref,
    v_ref,
    lse_ref,
    grad_one,
    grad_middle,
    grad_logit,
    normed,
    vec,
    wq,
    wk,
    wv,
    wo,
    *rest,
    image,
):
    grads, tokens_grad, sums, pulled = rest[-4:]
    slots = x_ref.shape[1]
    count = counts[image]
    pulled[...] = nt(grad_one[0], wo[...]).astype(BF16)
    lse = lse_ref[0].T
    inside = lax.broadcasted_iota(jnp.int32, (slots, 1), 0) < count
    masks = head_masks()
    for pair in range(HEADS // 2):
        at = slice(pair * PAIR, (pair + 1) * PAIR)
        queries, keys, values = q_ref[0, :, at], k_ref[0, :, at], v_ref[0, :, at]
        above = pulled[:, at]
        grad_q = grad_k = grad_v = None
        for e in range(2):
            h = 2 * pair + e
            own_keys = keys * masks[e]
            scores = nt(own_keys, queries) * SCORE_FACTOR - lse[h : h + 1]
            probs = jnp.exp2(jnp.where(inside, scores, MASKED))
            slope = probs * nt(values * masks[e], above)
            centre = row_sum(slope)
            low = (slope - probs * centre).astype(BF16)
            terms = (
                tn(low, own_keys),
                nn(low, queries * masks[e]),
                nn(probs.astype(BF16), above * masks[e]),
            )
            if e == 0:
                grad_q, grad_k, grad_v = terms
            else:
                grad_q, grad_k, grad_v = (
                    grad_q + terms[0],
                    grad_k + terms[1],
                    grad_v + terms[2],
                )
        grads[0, 0, :, at] = (grad_q * SCALE).astype(BF16)
        grads[1, 0, :, at] = (grad_k * SCALE).astype(BF16)
        grads[2, 0, :, at] = grad_v.astype(BF16)
    logit = grad_logit[0, :, :1]
    total = (
        nt(grads[0, 0], wq[...])
        + nt(grads[1, 0], wk[...])
        + nt(grads[2, 0], wv[...])
        + logit * vec[RW : RW + 1]
    )
    normal, scale = hat(x_ref[0].astype(F32))
    sums[0:1] = row_sum(grads[0, 0].astype(F32))
    sums[1:2] = row_sum(grads[2, 0].astype(F32))
    sums[2:3] = row_sum(total * normal)
    sums[3:4] = row_sum(total)
    sums[4:5] = row_sum(normed[0].astype(F32) * logit)
    back = hat_back(total * vec[G1 : G1 + 1], normal, scale)
    tokens_grad[0] = (back + grad_middle[0]).astype(BF16)


def run_attention_back(image, fields, vectors, weights, counts, before):
    images, slots, width = fields[0].shape
    at = lambda a: pl.BlockSpec((1,) + a.shape[1:], lambda i, c: (image, 0, 0))
    whole = lambda a: pl.BlockSpec(a.shape, lambda i, c: (0,) * a.ndim)
    args = [*fields, vectors, *weights]
    in_specs = [at(a) for a in fields] + [whole(a) for a in (vectors, *weights)]
    aliases = {}
    if before is not None:
        for n, array in enumerate(before):
            aliases[1 + len(args)] = n
            args.append(array)
            in_specs.append(pl.BlockSpec(memory_space=pl.ANY))
    shape = jax.ShapeDtypeStruct
    return pl.pallas_call(
        functools.partial(attention_back_kernel, image=image),
        grid_spec=pltpu.PrefetchScalarGridSpec(
            num_scalar_prefetch=1,
            grid=(1,),
            in_specs=in_specs,
            out_specs=[
                pl.BlockSpec((3, 1, slots, width), lambda i, c: (0, image, 0, 0)),
                pl.BlockSpec((1, slots, width), lambda i, c: (image, 0, 0)),
                pl.BlockSpec((8, width), lambda i, c: (0, 0)),
            ],
            scratch_shapes=[pltpu.VMEM((slots, width), BF16)],
        ),
        out_shape=[
            shape((3, images, slots, width), BF16),
            shape((images, slots, width), BF16),
            shape((8, width), F32),
        ],
        input_output_aliases=aliases,
        compiler_params=pltpu.CompilerParams(vmem_limit_bytes=VMEM),
        cost_estimate=pl.CostEstimate(
            flops=2 * slots * width * (4 * width + 5 * slots),
            bytes_accessed=12_000_000,
            transcendentals=HEADS * slots * slots,
        ),
        name="attention_backward",
    )(counts, *args)


def outer_kernel(half, normed, ctx, grads, grad_one, out):
    which = lax.rem(pl.program_id(0) + 2 * half[0], 4)

    @pl.when(which < 3)
    def _():
        out[0] = tn(normed[...], grads[0]).astype(BF16)

    @pl.when(which == 3)
    def _():
        out[0] = tn(ctx[...], grad_one[...]).astype(BF16)


def run_outer(half, normed, ctx, grads, grad_one):
    rows, width = normed.shape
    whole = lambda a: pl.BlockSpec(a.shape, lambda s, h: (0,) * a.ndim)
    return pl.pallas_call(
        outer_kernel,
        grid_spec=pltpu.PrefetchScalarGridSpec(
            num_scalar_prefetch=1,
            grid=(4,),
            in_specs=[
                whole(normed),
                whole(ctx),
                pl.BlockSpec(
                    (1, rows, width),
                    lambda s, h: (jnp.minimum(lax.rem(s + 2 * h[0], 4), 2), 0, 0),
                ),
                whole(grad_one),
            ],
            out_specs=pl.BlockSpec((1, width, width), lambda s, h: (s, 0, 0)),
        ),
        out_shape=jax.ShapeDtypeStruct((4, width, width), BF16),
        compiler_params=pltpu.CompilerParams(vmem_limit_bytes=VMEM),
        cost_estimate=pl.CostEstimate(
            flops=8 * rows * width * width, bytes_accessed=15_000_000, transcendentals=0
        ),
        name="outer",
    )(half, normed, ctx, grads, grad_one)


def bits_of(axis):
    size = lax.axis_size(axis)
    count = size.bit_length() - 1
    if size != 1 << count:
        raise ValueError("axis size")
    return [(axis, b) for b in range(count)]


def bit_of(step):
    axis, b = step
    return (lax.axis_index(axis) >> b) & 1


def swap(field, step):
    axis, b = step
    return lax.ppermute(field, axis, [(i, i ^ (1 << b)) for i in range(lax.axis_size(axis))])


def add_low(a, b):
    return (a.astype(F32) + b.astype(F32)).astype(BF16)


def halves(field, step):
    half = field.shape[0] // 2
    own = bit_of(step)
    return (
        lax.dynamic_slice_in_dim(field, (1 - own) * half, half),
        lax.dynamic_slice_in_dim(field, own * half, half),
    )


def scatter_sum(field, order):
    for step in order:
        if field.shape[0] % 2:
            field = add_low(field, swap(field, step))
            continue
        send, keep = halves(field, step)
        field = add_low(keep, swap(send, step))
    return field


def ordered(own, other, step, axis=0):
    return jnp.where(
        bit_of(step) == 0,
        jnp.concatenate([own, other], axis=axis),
        jnp.concatenate([other, own], axis=axis),
    )


def gather(field, order, rows):
    scattered = []
    for step in order:
        scattered.append(rows % 2 == 0)
        if rows % 2 == 0:
            rows //= 2
    for step, was in zip(reversed(order), reversed(scattered)):
        if was:
            field = ordered(field, swap(field, step), step)
    return field


def sum_over(field, order):
    return gather(scatter_sum(field, order), order, field.shape[0])


def to_images(field):
    return lax.all_to_all(field, "seq", split_axis=0, concat_axis=1, tiled=True)


def to_slots(field):
    return lax.all_to_all(field, "seq", split_axis=1, concat_axis=0, tiled=True)


def on_device(
    tokens,
    lengths,
    grad_out,
    query_weight,
    query_bias,
    key_weight,
    value_weight,
    value_bias,
    output_weight,
    output_bias,
    up_weight,
    up_bias,
    down_weight,
    down_bias,
    first_gain,
    first_shift,
    second_gain,
    second_shift,
    router_weight,
):
    tokens = to_images(tokens)
    grad_out = to_images(grad_out)
    images, slots, width = tokens.shape
    rows = images * slots
    lengths = lax.dynamic_slice_in_dim(lengths, lax.axis_index("seq") * images, images)
    counts = (lengths + 1) // 2
    vectors = [
        query_bias,
        value_bias,
        output_bias,
        first_gain,
        first_shift,
        second_gain,
        second_shift,
        router_weight,
        down_bias,
    ]
    vectors = jnp.pad(jnp.stack(vectors).astype(F32), ((0, 16 - len(vectors)), (0, 0)))
    flat = lambda field: field.reshape(rows, field.shape[-1])
    cube = lambda field: field.reshape(images, slots, field.shape[-1])

    weights = (query_weight, key_weight, value_weight, output_weight)
    normed, queries, keys, values, context, middle, one, second, gate, row, lse = run_attention(
        counts, tokens, vectors, *weights
    )

    first, *others = bits_of("dp")
    own = bit_of(first)
    mine, theirs = own.reshape(1), (1 - own).reshape(1)
    common = (flat(second), flat(grad_out), flat(row), up_weight, up_bias[None].astype(F32), down_weight)
    back, two, pulled, down_send, up_send, bias_send, back_sum = run_feed(theirs, *common)
    later = [back, two, pulled, flat(middle), flat(one), flat(gate), vectors]
    down_keep, up_keep, bias_keep, mixed, grad_middle, grad_one, grad_logit, sums = run_feed(
        mine, *common, later
    )
    mixed = to_slots(cube(mixed))
    down_part = add_low(down_keep, swap(down_send, first))
    up_part = add_low(up_keep, swap(up_send, first))
    seq_bits = bits_of("seq")
    order_a = others + seq_bits
    order_b = others[::-1] + seq_bits
    down_own = sum_over(down_part, order_a)
    up_own = sum_over(up_part, order_b)

    fields = (
        tokens,
        queries,
        keys,
        values,
        lse,
        cube(grad_one),
        cube(grad_middle),
        cube(grad_logit),
        normed,
    )
    before, small = None, 0.0
    for image in range(images):
        grads, tokens_grad, image_sums = run_attention_back(
            image, fields, vectors, weights, counts, before
        )
        before = (grads, tokens_grad)
        small = small + image_sums
    tokens_grad = to_slots(tokens_grad)
    outer = run_outer(
        theirs, flat(normed), flat(context), grads.reshape(3, rows, width), grad_one
    )
    four = outer.reshape(2, 2 * width, width)
    four = add_low(four[1], swap(four[0], first))
    third = four.shape[0] // 3
    orders = [order_a, order_b, seq_bits[:1] + others + seq_bits[1:]]
    four = jnp.concatenate(
        [sum_over(four[n * third : (n + 1) * third], orders[n]) for n in range(3)]
    )

    ratio = up_bias.shape[0] // width
    small = jnp.concatenate(
        [
            small[:5],
            sums[:3],
            back_sum,
            ordered(bias_keep, bias_send, first, 1).reshape(ratio, width),
        ]
    )
    small = jnp.sum(lax.all_gather(small, ("dp", "seq"), axis=0), axis=0)

    down_grad = ordered(down_own, swap(down_own, first), first).astype(F32)
    up_grad = ordered(up_own, swap(up_own, first), first, 1).astype(F32)
    four_other = swap(four, first)
    low, high = jnp.where(own == 0, four, four_other), jnp.where(own == 0, four_other, four)
    return (
        mixed,
        tokens_grad,
        low[:width].astype(F32),
        small[0],
        low[width:].astype(F32),
        high[:width].astype(F32),
        small[1],
        high[width:].astype(F32),
        small[7],
        up_grad,
        small[9:].reshape(-1),
        down_grad,
        small[8],
        small[2],
        small[3],
        small[5],
        small[6],
        small[4],
    )


def solution(mesh):
    rows = P("dp", "seq", None)
    in_specs = (rows, P("dp"), rows) + (P(),) * 16
    out_specs = (rows, rows) + (P(),) * 16
    return jax.shard_map(
        on_device, mesh=mesh, in_specs=in_specs, out_specs=out_specs, check_vma=False
    )
```

```python
import functools
import math

import jax
import jax.numpy as jnp
from jax import lax
from jax.experimental import pallas as pl
from jax.experimental.pallas import tpu as pltpu
from jax.sharding import PartitionSpec as P

HEADS = 12
HEAD_DIM = 64
EPSILON = 1e-06
PAIR = 2 * HEAD_DIM
LANES = 128
SCALE = HEAD_DIM ** (-0.5)
SCORE_FACTOR = SCALE * math.log2(math.e)
ROOT_HALF = math.sqrt(0.5)
DENSITY = 1.0 / math.sqrt(2.0 * math.pi)
BELL = -0.5 * math.log2(math.e)
MASKED = -1e30
TILE = 512
MIB = 1024 * 1024
F32 = jnp.float32
BF16 = jnp.bfloat16

QB, VB, OB, G1, S1, G2, S2, RW, DB = range(9)


def cost(microseconds):
    return pl.CostEstimate(
        flops=microseconds * 1_150_000_000, bytes_accessed=1_000_000, transcendentals=0
    )


def nn(a, b):
    return lax.dot_general(a, b, (((1,), (0,)), ((), ())), preferred_element_type=F32)


def nt(a, b):
    return lax.dot_general(a, b, (((1,), (1,)), ((), ())), preferred_element_type=F32)


def tn(a, b):
    return lax.dot_general(a, b, (((0,), (0,)), ((), ())), preferred_element_type=F32)


def hat(field):
    mean = jnp.mean(field, axis=-1, keepdims=True)
    centred = field - mean
    spread = jnp.mean(centred * centred, axis=-1, keepdims=True)
    scale = lax.rsqrt(spread + EPSILON)
    return centred * scale, scale


def hat_back(grad, normal, scale):
    first = jnp.mean(grad, axis=-1, keepdims=True)
    second = jnp.mean(grad * normal, axis=-1, keepdims=True)
    return scale * (grad - first - normal * second)


def row_sum(field):
    return jnp.sum(field, axis=0, keepdims=True)


def head_masks():
    lane = lax.broadcasted_iota(jnp.int32, (1, PAIR), 1)
    return [
        jnp.where(lane < HEAD_DIM, 1.0, 0.0).astype(BF16),
        jnp.where(lane < HEAD_DIM, 0.0, 1.0).astype(BF16),
    ]


def block_at(me, distance, size):
    return pl.ds(pl.multiple_of(jnp.bitwise_xor(me, distance) * size, 16), size)


def attention_kernel(info, *refs, image, parts):
    came, (vec, wq, wk, wv, wo) = refs[:parts], refs[parts : parts + 5]
    (
        x_ref,
        normed_ref,
        q_ref,
        k_ref,
        v_ref,
        ctx_ref,
        middle_ref,
        one_ref,
        second_ref,
        gate_ref,
        row_ref,
        lse_ref,
    ) = refs[-12:]
    slots = x_ref.shape[1]
    size = slots // parts
    count = info[1 + image]
    for distance in range(parts):
        x_ref[0, block_at(info[0], distance, size), :] = came[distance][0]
    x = x_ref[0].astype(F32)
    normal, _ = hat(x)
    normed = (normal * vec[G1 : G1 + 1] + vec[S1 : S1 + 1]).astype(BF16)
    normed_ref[0] = normed
    logit = jnp.sum(normed.astype(F32) * vec[RW : RW + 1], axis=-1, keepdims=True)
    gate = jax.nn.sigmoid(logit)
    inside = lax.broadcasted_iota(jnp.int32, (slots, 1), 0) < count
    row = jnp.where(inside, gate, 0.0)
    gate_ref[0] = jnp.broadcast_to(gate, (slots, LANES))
    row_ref[0] = jnp.broadcast_to(row, (slots, LANES))
    q_ref[0] = (nn(normed, wq[...]) + vec[QB : QB + 1]).astype(BF16)
    k_ref[0] = nn(normed, wk[...]).astype(BF16)
    v_ref[0] = (nn(normed, wv[...]) + vec[VB : VB + 1]).astype(BF16)
    key_mask = jnp.where(
        lax.broadcasted_iota(jnp.int32, (1, slots), 1) < count, 0.0, MASKED
    )
    masks = head_masks()
    lane = lax.broadcasted_iota(jnp.int32, (1, LANES), 1)
    ones = jnp.ones((slots, LANES), BF16)
    lse = jnp.zeros((slots, LANES), F32)
    for pair in range(HEADS // 2):
        at = slice(pair * PAIR, (pair + 1) * PAIR)
        queries = q_ref[0, :, at]
        keys = k_ref[0, :, at]
        values = jnp.concatenate([v_ref[0, :, at], ones], axis=1)
        halves = []
        for e in range(2):
            scores = nt(queries * masks[e], keys) * SCORE_FACTOR + key_mask
            top = jnp.max(scores, axis=-1, keepdims=True)
            expo = jnp.exp2(scores - top).astype(BF16)
            mixed = nn(expo, values)
            total = mixed[:, PAIR:]
            halves.append(mixed[:, :PAIR] / total)
            lse = jnp.where(lane == 2 * pair + e, top + jnp.log2(total), lse)
        low = jnp.where(lane < HEAD_DIM, halves[0], halves[1])
        ctx_ref[0, :, at] = low.astype(BF16)
    lse_ref[0] = lse
    one = nn(ctx_ref[0], wo[...]) + vec[OB : OB + 1]
    one_ref[0] = one.astype(BF16)
    middle = x + row * one
    middle_ref[0] = middle
    again, _ = hat(middle)
    second_ref[0] = (again * vec[G2 : G2 + 1] + vec[S2 : S2 + 1]).astype(BF16)


def chained(args, in_specs, before):
    aliases = {}
    for n, array in enumerate(before or ()):
        aliases[1 + len(args)] = n
        args.append(array)
        in_specs.append(pl.BlockSpec(memory_space=pl.ANY))
    return aliases


def run_attention(image, images, info, own, came, vectors, weights, before):
    parts = 1 + len(came)
    size, width = own.shape[1:]
    slots = parts * size
    whole = lambda a: pl.BlockSpec(a.shape, lambda i, c: (0,) * a.ndim)
    args = [own, *came, vectors, *weights]
    in_specs = [pl.BlockSpec((1, size, width), lambda i, c: (c[0] * images + image, 0, 0))]
    in_specs += [whole(a) for a in args[1:]]
    aliases = chained(args, in_specs, before)
    outs = [(width, BF16)] * 6 + [(width, F32)] + [(width, BF16)] * 2 + [(LANES, F32)] * 3
    return pl.pallas_call(
        functools.partial(attention_kernel, image=image, parts=parts),
        grid_spec=pltpu.PrefetchScalarGridSpec(
            num_scalar_prefetch=1,
            grid=(1,),
            in_specs=in_specs,
            out_specs=[
                pl.BlockSpec((1, slots, lanes), lambda i, c: (image, 0, 0)) for lanes, _ in outs
            ],
        ),
        out_shape=[jax.ShapeDtypeStruct((images, slots, lanes), t) for lanes, t in outs],
        input_output_aliases=aliases,
        compiler_params=pltpu.CompilerParams(vmem_limit_bytes=24 * MIB),
        cost_estimate=cost(8),
        name="attention_forward",
    )(info, *args)


def feed_body(second, flipped, back, up, bias, down, two, pulled, down_grad, up_grad, bias_grad):
    hidden = nn(second[...], up[...]) + bias[...]
    phi = 0.5 + 0.5 * lax.erf(hidden * ROOT_HALF)
    density = DENSITY * jnp.exp2(hidden * hidden * BELL)
    active = (hidden * phi).astype(BF16)
    slope = phi + hidden * density
    two[...] += nn(active, down[...])
    low = (nt(back[...], down[...]) * slope).astype(BF16)
    bias_grad[...] = row_sum(low.astype(F32))
    pulled[...] += nt(low, up[...])
    down_grad[...] = tn(active, back[...]).astype(BF16)
    up_grad[...] = nn(flipped[...], low).astype(BF16)


def feed_first_kernel(info, second, row, up, bias, down, *refs, images):
    *came, grad_out, back, flipped, back_sum, two, pulled, down_grad, up_grad, bias_grad = refs

    @pl.when(pl.program_id(0) == 0)
    def _():
        parts = len(came)
        size = came[0].shape[1]
        slots = parts * size
        total = jnp.zeros(back_sum.shape, F32)
        for image in range(images):
            for distance in range(parts):
                start = jnp.bitwise_xor(info[0], distance) * size + image * slots
                at = pl.ds(pl.multiple_of(start, 16), size)
                upstream = came[distance][image]
                grad_out[at, :] = upstream
                value = (row[at, :1] * upstream.astype(F32)).astype(BF16)
                back[at, :] = value
                total = total + row_sum(value.astype(F32))
        back_sum[...] = total
        flipped[...] = second[...].T
        two[...] = jnp.zeros_like(two)
        pulled[...] = jnp.zeros_like(pulled)

    feed_body(second, flipped, back, up, bias, down, two, pulled, down_grad, up_grad, bias_grad)


def feed_second_kernel(
    info,
    second,
    row,
    up,
    bias,
    down,
    back,
    flipped,
    two_in,
    pulled_in,
    two,
    pulled,
    down_grad,
    up_grad,
    bias_grad,
):
    @pl.when(pl.program_id(0) == 0)
    def _():
        two[...] = two_in[...]
        pulled[...] = pulled_in[...]

    feed_body(second, flipped, back, up, bias, down, two, pulled, down_grad, up_grad, bias_grad)


def run_feed(info, second, row, up, bias, down, images, came=None, before=None):
    rows, width = second.shape
    units = up.shape[1] // 2
    tiles = units // TILE
    whole = lambda a: pl.BlockSpec(a.shape, lambda t, c: (0,) * len(a.shape))
    shape = jax.ShapeDtypeStruct
    in_specs = [
        whole(second),
        whole(row),
        pl.BlockSpec((width, TILE), lambda t, c: (0, c[1] * tiles + t)),
        pl.BlockSpec((1, TILE), lambda t, c: (0, c[1] * tiles + t)),
        pl.BlockSpec((TILE, width), lambda t, c: (c[1] * tiles + t, 0)),
    ]
    field = lambda dtype: shape((rows, width), dtype)
    args = [second, row, up, bias, down]
    outs = [field(F32), field(F32)]
    if came is not None:
        body = functools.partial(feed_first_kernel, images=images)
        in_specs += [pl.BlockSpec((images,) + came[0].shape[1:], lambda t, c: (c[0], 0, 0))]
        in_specs += [whole(a) for a in came[1:]]
        args += came
        outs = [field(BF16), field(BF16), shape((width, rows), BF16), shape((1, width), F32)] + outs
    else:
        body = feed_second_kernel
        in_specs += [whole(a) for a in before]
        args += before
    tile_outs = [shape((units, width), BF16), shape((width, units), BF16), shape((1, units), F32)]
    return pl.pallas_call(
        body,
        grid_spec=pltpu.PrefetchScalarGridSpec(
            num_scalar_prefetch=1,
            grid=(tiles,),
            in_specs=in_specs,
            out_specs=[whole(o) for o in outs]
            + [
                pl.BlockSpec((TILE, width), lambda t, c: (t, 0)),
                pl.BlockSpec((width, TILE), lambda t, c: (0, t)),
                pl.BlockSpec((1, TILE), lambda t, c: (0, t)),
            ],
        ),
        out_shape=outs + tile_outs,
        compiler_params=pltpu.CompilerParams(vmem_limit_bytes=48 * MIB),
        cost_estimate=cost(21),
        name="feed_first" if came is not None else "feed_second",
    )(info, *args)


def middle_kernel(
    info, pulled, grad_out, two, middle, one, row, gate, vec, total_ref, low_ref, logit_ref, sums, *rest
):
    *mixed, result = rest
    upstream = grad_out[...].astype(F32)
    weight = row[:, :1]
    branch_two = two[...] + vec[DB : DB + 1]
    centre = middle[...]
    result[...] = (centre + weight * branch_two).astype(BF16)
    size = mixed[0].shape[1]
    for pair in range(len(mixed) // 2):

        @pl.when(pl.program_id(1) == pair)
        def _(pair=pair):
            low_bit = jnp.bitwise_and(info[0], 1)
            for e in range(2):
                at = pl.ds(pl.multiple_of(jnp.bitwise_xor(low_bit, e) * size, 16), size)
                mixed[2 * pair + e][0] = result[at, :]

    normal, scale = hat(centre)
    grad = pulled[...]
    total = hat_back(grad * vec[G2 : G2 + 1], normal, scale) + upstream
    total_ref[...] = total.astype(BF16)
    low = (weight * total).astype(BF16)
    low_ref[...] = low
    gated = jnp.sum(
        upstream * branch_two + total * one[...].astype(F32), axis=-1, keepdims=True
    )
    logit_ref[...] = weight * (1.0 - gate[...]) * gated

    @pl.when(jnp.logical_and(pl.program_id(0) == 0, pl.program_id(1) == 0))
    def _():
        sums[...] = jnp.zeros_like(sums)

    sums[0:1] += row_sum(grad * normal)
    sums[1:2] += row_sum(grad)
    sums[2:3] += row_sum(low.astype(F32))


def run_middle(info, fields, vectors, images, parts):
    rows, width = fields[0].shape
    size = rows // images // parts
    block = 2 * size
    place = lambda i, p, c: (i * (parts // 2) + jnp.bitwise_xor(lax.div(c[0], 2), p), 0)
    at = lambda a: pl.BlockSpec((block, a.shape[1]), place)
    shape = jax.ShapeDtypeStruct
    outs = [shape((rows, width), BF16), shape((rows, width), BF16), shape((rows, LANES), F32)]
    mixed = pl.BlockSpec((1, size, width), lambda i, d, c: (i, 0, 0))
    return pl.pallas_call(
        middle_kernel,
        grid_spec=pltpu.PrefetchScalarGridSpec(
            num_scalar_prefetch=1,
            grid=(images, parts // 2),
            in_specs=[at(a) for a in fields] + [pl.BlockSpec(vectors.shape, lambda i, d, c: (0, 0))],
            out_specs=[at(o) for o in outs]
            + [pl.BlockSpec((8, width), lambda i, d, c: (0, 0))]
            + [mixed] * parts,
            scratch_shapes=[pltpu.VMEM((block, width), BF16)],
        ),
        out_shape=outs + [shape((8, width), F32)] + [shape((images, size, width), BF16)] * parts,
        compiler_params=pltpu.CompilerParams(vmem_limit_bytes=24 * MIB),
        cost_estimate=cost(8),
        name="middle",
    )(info, *fields, vectors)


def attention_back_kernel(
    info,
    x_ref,
    q_ref,
    k_ref,
    v_ref,
    lse_ref,
    grad_one,
    grad_middle,
    grad_logit,
    normed,
    vec,
    wq,
    wk,
    wv,
    wo,
    *rest,
    image,
    parts,
):
    grads, *tokens_grad, sums, pulled, tokens_back = rest[-5 - parts + 1 :]
    slots = x_ref.shape[1]
    count = info[1 + image]
    pulled[...] = nt(grad_one[0], wo[...]).astype(BF16)
    lse = lse_ref[0].T
    inside = lax.broadcasted_iota(jnp.int32, (slots, 1), 0) < count
    masks = head_masks()
    for pair in range(HEADS // 2):
        at = slice(pair * PAIR, (pair + 1) * PAIR)
        queries, keys, values = q_ref[0, :, at], k_ref[0, :, at], v_ref[0, :, at]
        above = pulled[:, at]
        grad_q = grad_k = grad_v = None
        for e in range(2):
            h = 2 * pair + e
            own_keys = keys * masks[e]
            scores = nt(own_keys, queries) * SCORE_FACTOR - lse[h : h + 1]
            probs = jnp.exp2(jnp.where(inside, scores, MASKED))
            slope = probs * nt(values * masks[e], above)
            centre = row_sum(slope)
            low = (slope - probs * centre).astype(BF16)
            terms = (
                tn(low, own_keys),
                nn(low, queries * masks[e]),
                nn(probs.astype(BF16), above * masks[e]),
            )
            if e == 0:
                grad_q, grad_k, grad_v = terms
            else:
                grad_q, grad_k, grad_v = (
                    grad_q + terms[0],
                    grad_k + terms[1],
                    grad_v + terms[2],
                )
        grads[0, :, at] = (grad_q * SCALE).astype(BF16)
        grads[1, :, at] = (grad_k * SCALE).astype(BF16)
        grads[2, :, at] = grad_v.astype(BF16)
    logit = grad_logit[0, :, :1]
    total = (
        nt(grads[0], wq[...])
        + nt(grads[1], wk[...])
        + nt(grads[2], wv[...])
        + logit * vec[RW : RW + 1]
    )
    normal, scale = hat(x_ref[0].astype(F32))
    sums[0:1] = row_sum(grads[0].astype(F32))
    sums[1:2] = row_sum(grads[2].astype(F32))
    sums[2:3] = row_sum(total * normal)
    sums[3:4] = row_sum(total)
    sums[4:5] = row_sum(normed[0].astype(F32) * logit)
    back = hat_back(total * vec[G1 : G1 + 1], normal, scale)
    tokens_back[...] = (back + grad_middle[0].astype(F32)).astype(BF16)
    for distance in range(parts):
        tokens_grad[distance][0] = tokens_back[block_at(info[0], distance, slots // parts), :]


def run_attention_back(image, info, fields, vectors, weights, parts):
    images, slots, width = fields[0].shape
    at = lambda a: pl.BlockSpec((1,) + a.shape[1:], lambda i, c: (image, 0, 0))
    whole = lambda a: pl.BlockSpec(a.shape, lambda i, c: (0,) * a.ndim)
    args = [*fields, vectors, *weights]
    in_specs = [at(a) for a in fields] + [whole(a) for a in (vectors, *weights)]
    shape = jax.ShapeDtypeStruct
    size = slots // parts
    return pl.pallas_call(
        functools.partial(attention_back_kernel, image=image, parts=parts),
        grid_spec=pltpu.PrefetchScalarGridSpec(
            num_scalar_prefetch=1,
            grid=(1,),
            in_specs=in_specs,
            out_specs=[pl.BlockSpec((3, slots, width), lambda i, c: (0, 0, 0))]
            + [pl.BlockSpec((1, size, width), lambda i, c: (0, 0, 0))] * parts
            + [pl.BlockSpec((8, width), lambda i, c: (0, 0))],
            scratch_shapes=[pltpu.VMEM((slots, width), BF16)] * 2,
        ),
        out_shape=[shape((3, slots, width), BF16)]
        + [shape((1, size, width), BF16)] * parts
        + [shape((8, width), F32)],
        compiler_params=pltpu.CompilerParams(vmem_limit_bytes=28 * MIB),
        cost_estimate=cost(11),
        name="attention_backward",
    )(info, *args)


def shared_out(tiles, step):
    return jnp.minimum(step, tiles - 1), jnp.maximum(step - tiles, 0)


def outer_kernel(info, normed, ctx, grad_one, *refs, images):
    grads, (send, keep, flipped, joined) = refs[:images], refs[images:]
    step = pl.program_id(0)
    half = pl.num_programs(0) // 2
    which = lax.rem(step + half * (1 - info[1]), 2 * half)

    @pl.when(step == 0)
    def _():
        flipped[...] = normed[...].T

    @pl.when(which < 3)
    def _():
        slots = grads[0].shape[1]
        for image in range(images):
            joined[image * slots : (image + 1) * slots] = grads[image][0]

    for out, now in ((send, step < half), (keep, step >= half)):

        @pl.when(jnp.logical_and(now, which < 3))
        def _(out=out):
            out[...] = nn(flipped[...], joined[...]).astype(BF16)

        @pl.when(jnp.logical_and(now, which == 3))
        def _(out=out):
            out[...] = tn(ctx[...], grad_one[...]).astype(BF16)


def run_outer(info, normed, ctx, grad_one, grads):
    rows, width = normed.shape
    images = len(grads)
    whole = lambda a: pl.BlockSpec(a.shape, lambda s, c: (0,) * a.ndim)
    return pl.pallas_call(
        functools.partial(outer_kernel, images=images),
        grid_spec=pltpu.PrefetchScalarGridSpec(
            num_scalar_prefetch=1,
            grid=(4,),
            in_specs=[
                whole(normed),
                whole(ctx),
                whole(grad_one),
            ]
            + [
                pl.BlockSpec(
                    (1, rows // images, width),
                    lambda s, c: (jnp.minimum(lax.rem(s + 2 * (1 - c[1]), 4), 2), 0, 0),
                )
            ]
            * images,
            out_specs=[
                pl.BlockSpec((width, width), lambda s, c, n=n: (shared_out(2, s)[n], 0))
                for n in range(2)
            ],
            scratch_shapes=[pltpu.VMEM((width, rows), BF16), pltpu.VMEM((rows, width), BF16)],
        ),
        out_shape=[jax.ShapeDtypeStruct((2 * width, width), BF16)] * 2,
        compiler_params=pltpu.CompilerParams(vmem_limit_bytes=24 * MIB),
        cost_estimate=cost(9),
        name="outer",
    )(info, normed, ctx, grad_one, *grads)


def bits_of(axis):
    size = lax.axis_size(axis)
    count = size.bit_length() - 1
    if size != 1 << count:
        raise ValueError("axis size")
    return [(axis, b) for b in range(count)]


def bit_of(step):
    axis, b = step
    return (lax.axis_index(axis) >> b) & 1


def swap(field, step):
    axis, b = step
    return lax.ppermute(field, axis, [(i, i ^ (1 << b)) for i in range(lax.axis_size(axis))])


def add_low(a, b):
    return (a.astype(F32) + b.astype(F32)).astype(BF16)


def halves(field, step):
    half = field.shape[0] // 2
    own = bit_of(step)
    return (
        lax.dynamic_slice_in_dim(field, (1 - own) * half, half),
        lax.dynamic_slice_in_dim(field, own * half, half),
    )


def ordered(own, other, step, axis=0):
    return jnp.where(
        bit_of(step) == 0,
        jnp.concatenate([own, other], axis=axis),
        jnp.concatenate([other, own], axis=axis),
    )


def spread_kernel(info, own, other, out):
    @pl.when(pl.program_id(0) == 0)
    def _():
        out[...] = own[...].astype(F32)

    @pl.when(pl.program_id(0) == 1)
    def _():
        out[...] = other[...].astype(F32)


def run_spread(info, own, other, axis):
    rows, cols = own.shape
    cuts = 2
    block = (rows // cuts, cols)
    place = lambda h, b: (b, h) if axis else (h * cuts + b, 0)
    still = cuts - 1
    return pl.pallas_call(
        spread_kernel,
        grid_spec=pltpu.PrefetchScalarGridSpec(
            num_scalar_prefetch=1,
            grid=(2, cuts),
            in_specs=[
                pl.BlockSpec(block, lambda h, b, c: (jnp.where(h == 0, b, still), 0)),
                pl.BlockSpec(block, lambda h, b, c: (jnp.where(h == 0, 0, b), 0)),
            ],
            out_specs=pl.BlockSpec(block, lambda h, b, c: place(jnp.bitwise_xor(h, c[1]), b)),
        ),
        out_shape=jax.ShapeDtypeStruct((rows * (2 - axis), cols * (1 + axis)), F32),
        compiler_params=pltpu.CompilerParams(vmem_limit_bytes=24 * MIB),
        cost_estimate=cost(7),
        name="spread",
    )(info, own, other)


def split_kernel(info, own, other, *outs, cuts):
    step = pl.program_id(0)
    for g in range(2):
        for w in range(2):
            start = (jnp.bitwise_xor(g, info[1]) * 2 + w) * cuts
            now = jnp.logical_and(step >= start, step < start + cuts)
            for source, near in ((own, step < 2 * cuts), (other, step >= 2 * cuts)):

                @pl.when(jnp.logical_and(now, near))
                def _(source=source, out=outs[2 * g + w]):
                    out[...] = source[...].astype(F32)


def run_split(info, own, other):
    rows, width = own.shape
    cuts = 1
    side = rows // 2
    block = (side // cuts, width)

    def place(t, c, g, w):
        start = (jnp.bitwise_xor(g, c[1]) * 2 + w) * cuts
        return jnp.clip(t - start, 0, cuts - 1), 0

    return pl.pallas_call(
        functools.partial(split_kernel, cuts=cuts),
        grid_spec=pltpu.PrefetchScalarGridSpec(
            num_scalar_prefetch=1,
            grid=(4 * cuts,),
            in_specs=[
                pl.BlockSpec(block, lambda t, c: (jnp.minimum(t, 2 * cuts - 1), 0)),
                pl.BlockSpec(block, lambda t, c: (jnp.maximum(t - 2 * cuts, 0), 0)),
            ],
            out_specs=[
                pl.BlockSpec(block, functools.partial(place, g=g, w=w))
                for g in range(2)
                for w in range(2)
            ],
        ),
        out_shape=[jax.ShapeDtypeStruct((side, width), F32)] * 4,
        compiler_params=pltpu.CompilerParams(vmem_limit_bytes=24 * MIB),
        cost_estimate=cost(8),
        name="split",
    )(info, own, other)


def swap_far(field, distance):
    size = lax.axis_size("seq")
    return lax.ppermute(field, "seq", [(i, i ^ distance) for i in range(size)])


class Stage:
    def __init__(self, sends, moves, finish):
        self.sends, self.moves, self.finish = sends, moves, finish


def move_by(step):
    return lambda field: swap(field, step)


def move_far(distance):
    return lambda field: swap_far(field, distance)


def scatter_stage(fields, steps):
    pieces = [halves(f, s) for f, s in zip(fields, steps)]
    return Stage(
        [p[0] for p in pieces],
        [move_by(s) for s in steps],
        lambda came: [add_low(p[1], c) for p, c in zip(pieces, came)],
    )


def gather_stage(fields, steps, axis=0):
    return Stage(
        fields,
        [move_by(s) for s in steps],
        lambda came: [ordered(f, c, s, axis) for f, c, s in zip(fields, came, steps)],
    )


def begin(stages, *gates):
    sends = [s for stage in stages for s in stage.sends]
    results = lax.optimization_barrier((*gates, *sends))
    moves = [m for stage in stages for m in stage.moves]
    came = [m(s) for m, s in zip(moves, results[len(gates) :])]
    return list(results[: len(gates)]), (stages, came)


def end(pending, *markers):
    stages, came = pending
    came = list(lax.optimization_barrier((*came, *markers))[: len(came)])
    left, results = came, []
    for stage in stages:
        count = len(stage.sends)
        results.append(stage.finish(left[:count]))
        left = left[count:]
    return (*results, came)


def exchange(*stages):
    return end(begin(stages)[1])[:-1]


def place_kernel(info, *refs, counts):
    *parts, out = refs
    at = 0
    for distance, count in enumerate(counts):

        @pl.when(pl.program_id(0) == distance)
        def _(now=parts[at : at + count]):
            rows = 0
            for part in now:
                out[rows : rows + part.shape[0]] = part[...]
                rows += part.shape[0]

        at += count


def run_place(info, parts):
    size, width = parts[0][0].shape[1:]
    images = sum(p.shape[0] for p in parts[0])
    args = [p for group in parts for p in group]
    return pl.pallas_call(
        functools.partial(place_kernel, counts=[len(group) for group in parts]),
        grid_spec=pltpu.PrefetchScalarGridSpec(
            num_scalar_prefetch=1,
            grid=(len(parts),),
            in_specs=[pl.BlockSpec(a.shape, lambda d, c: (0, 0, 0)) for a in args],
            out_specs=pl.BlockSpec(
                (images, size, width), lambda d, c: (jnp.bitwise_xor(c[0], d), 0, 0)
            ),
        ),
        out_shape=jax.ShapeDtypeStruct((len(parts) * images, size, width), BF16),
        compiler_params=pltpu.CompilerParams(vmem_limit_bytes=24 * MIB),
        cost_estimate=cost(3),
        name="place",
    )(info, *args)


def after(value, *others):
    return lax.optimization_barrier((value, *others))[0]


def on_device(
    tokens,
    lengths,
    grad_out,
    query_weight,
    query_bias,
    key_weight,
    value_weight,
    value_bias,
    output_weight,
    output_bias,
    up_weight,
    up_bias,
    down_weight,
    down_bias,
    first_gain,
    first_shift,
    second_gain,
    second_shift,
    router_weight,
):
    parts = lax.axis_size("seq")
    me = lax.axis_index("seq").astype(jnp.int32)
    group, size, width = tokens.shape
    images = group // parts
    slots = parts * size
    rows = images * slots
    distances = range(1, parts)
    came = []
    for image in range(images):
        sends = [
            lax.dynamic_index_in_dim(tokens, (me ^ d) * images + image, keepdims=True)
            for d in distances
        ]
        if image:
            sends = [after(send, *came[0]) for send in sends]
        came.append([swap_far(send, d) for send, d in zip(sends, distances)])
    sends = [
        after(lax.dynamic_slice_in_dim(grad_out, (me ^ d) * images, images), *came[min(1, images - 1)])
        for d in distances
    ]
    grad_came = [grad_out] + [swap_far(send, d) for send, d in zip(sends, distances)]

    lengths = lax.dynamic_slice_in_dim(lengths, me * images, images)
    info = jnp.concatenate([me.reshape(1), (lengths + 1) // 2])
    vectors = [
        query_bias,
        value_bias,
        output_bias,
        first_gain,
        first_shift,
        second_gain,
        second_shift,
        router_weight,
        down_bias,
    ]
    vectors = jnp.pad(jnp.stack(vectors).astype(F32), ((0, 16 - len(vectors)), (0, 0)))
    flat = lambda field: field.reshape(rows, field.shape[-1])
    cube = lambda field: field.reshape(images, slots, field.shape[-1])

    weights = (query_weight, key_weight, value_weight, output_weight)
    before = None
    for image in range(images):
        before = run_attention(
            image, images, info, tokens, came[image], vectors, weights, before
        )
    x, normed, queries, keys, values, context, middle, one, second, gate, row, lse = before

    first, *others = bits_of("dp")
    crossed = others[::-1]
    own = bit_of(first)
    mine = jnp.stack([me, own])
    far = [move_far(d) for d in distances]

    seq_bits = bits_of("seq")
    pair = lambda n: (others[n], crossed[n])
    core = lambda sent, kept: Stage([sent], [move_by(first)], lambda came: [add_low(kept, came[0])])
    join = lambda fields: [jnp.concatenate(fields)]

    common = (flat(second), flat(row), up_weight, up_bias[None].astype(F32), down_weight, images)
    theirs = after(jnp.stack([me, 1 - own]), *grad_came[1:])
    grad_out, back, flipped, back_sum, two, pulled, down_send, up_send, bias_send = run_feed(
        theirs, *common, came=grad_came
    )
    (gated,), pending = begin(
        [Stage([down_send, up_send], [move_by(first)] * 2, lambda came: came)], mine
    )
    two, pulled, down_keep, up_keep, bias_keep = run_feed(
        gated, *common, before=[back, flipped, two, pulled]
    )
    feed_came, came = end(pending, bias_keep)
    feed = [add_low(down_keep, feed_came[0]), add_low(up_keep, feed_came[1])]

    (info,), pending = begin([scatter_stage(feed, pair(0))], after(info, *came))
    middle_fields = (pulled, grad_out, two, flat(middle), flat(one), flat(row), flat(gate))
    grad_middle, grad_one, grad_logit, sums, *mixed = run_middle(
        info, middle_fields, vectors, images, parts
    )
    mixed_came = [begin([Stage([part], [move], list)])[1] for part, move in zip(mixed[1:], far)]

    fields = (
        x,
        queries,
        keys,
        values,
        lse,
        cube(grad_one),
        cube(grad_middle),
        cube(grad_logit),
        normed,
    )
    tokens_parts = []
    left = [("xy", n) for n in range(1, len(others))] + [("z", s) for s in seq_bits]

    def feed_stage(feed):
        kind, step = left.pop(0)
        if kind == "xy":
            return scatter_stage(feed, pair(step))
        if len(feed) == 2:
            feed = [jnp.concatenate([feed[0], feed[1].reshape(-1, width)])]
        return scatter_stage(feed, [step])

    grads, gated = [], info
    for image in range(images):
        image_grads, *part, image_sums = run_attention_back(
            image, gated, fields, vectors, weights, parts
        )
        grads.append(image_grads)
        tokens_parts.append(part)
        small = small + image_sums if image else image_sums
        if image < len(mixed_came):
            (mixed_came[image],), extra = end(mixed_came[image], image_sums)
        else:
            extra = []
        if image < images - 1:
            gated = after(gated, *extra)
        if image == images - 2 or images == 1:
            feed, came = end(pending, image_sums)
            while len(left) > 3:
                (feed,) = exchange(feed_stage(feed))
            (gated,), pending = begin([feed_stage(feed)], after(gated, *came))
    feed, came = end(pending, image_sums)
    (gated,), pending = begin([feed_stage(feed)], after(mine, *came, *extra))
    four_send, four_keep = run_outer(gated, flat(normed), flat(context), grad_one, grads)
    feed, came = end(pending, four_keep[:8])
    while len(left) > 1:
        (feed,) = exchange(feed_stage(feed))

    small = jnp.concatenate(
        [
            small[:5],
            sums[:3],
            back_sum,
            ordered(bias_keep, bias_send, first, 1).reshape(-1, width),
        ]
    )
    small_rows = small.shape[0]
    cut = 1 << (len(others) + len(seq_bits))
    small = jnp.pad(small, ((0, -small_rows % cut), (0, 0)))

    def four_parts(came):
        total = add_low(four_keep, came[0])
        half = total.shape[0] // 2
        return [
            jnp.concatenate([total[:half], (small + came[1]).astype(BF16)]),
            total[half:],
        ]

    def feed_back_stage(step, feed):
        kind, step = step
        if kind == "last":
            return feed_stage(feed)
        if kind == "z":
            return gather_stage(feed, [step])
        if len(feed) == 1:
            half = feed[0].shape[0] // 2
            feed = [feed[0][:half], feed[0][half:].reshape(-1, up_keep.shape[1])]
        if kind == "xy":
            return gather_stage(feed, pair(step))
        return Stage(feed, [move_by(first)] * 2, lambda came: list(zip(feed, came)))

    feed_left = [("last", None)] * len(left) + [("z", s) for s in reversed(seq_bits)]
    feed_left += [("xy", n) for n in reversed(range(len(others)))] + [("core", first)]
    four_left = [("core", first)] + [("cut", n) for n in range(len(others))]
    four_left += [("join", s) for s in seq_bits] + [("bind", s) for s in reversed(seq_bits)]
    four_left += [("grow", n) for n in reversed(range(len(others)))]
    count = len(feed_left)
    spans = [(0, 0), (1, 1), (2, 2), (3, 4), (5, 6), (7, 7)]
    if count != len(spans):
        spans = [(n, n) for n in range(count)]
    stages = len(four_left)
    four, feed_pending, widths, came = None, None, None, None
    tokens_own = [part[0] for part in tokens_parts]
    tokens_spans = [(3, 4), (6, 7), (8, 8)][: len(far)]
    tokens_spans += [(0, stages)] * (len(far) - len(tokens_spans))
    tokens_pending, tokens_came = {}, {}
    for n, (kind, step) in enumerate(four_left):
        if kind == "core":
            stage = Stage([four_send, small], [move_by(first)] * 2, four_parts)
        elif kind == "cut":
            stage = scatter_stage(four, pair(step))
        elif kind == "join":
            if len(four) == 2:
                widths = four[0].shape[0]
                four = join(four)
            stage = scatter_stage(four, [step])
        elif kind == "bind":
            stage = gather_stage(four, [step])
        else:
            if len(four) == 1:
                four = [four[0][:widths], four[0][widths:]]
            stage = gather_stage(four, pair(step))
        starts = [a for a, _ in spans]
        if n in starts:
            more = feed_back_stage(feed_left[starts.index(n)], feed)
            _, (_, moving) = begin([stage, more])
            count = len(stage.sends)
            pending, feed_pending = ([stage], moving[:count]), ([more], moving[count:])
        else:
            _, pending = begin([stage])
        markers = []
        if n == 1:
            for m in range(images, len(mixed_came)):
                (mixed_came[m],), _ = end(mixed_came[m])
            mixed = run_place(after(info, *came), [[mixed[0]]] + [[c] for c in mixed_came])
            markers = [mixed]
        if n == stages - 1:
            down, up = (
                run_spread(after(mine, *came), *pair_of, axis) for axis, pair_of in enumerate(feed)
            )
            markers = [down, up]
        for m, (a, b) in enumerate(tokens_spans):
            if a == n:
                joined = jnp.concatenate([part[m + 1] for part in tokens_parts])
                if came is not None:
                    joined = after(joined, *came)
                tokens_pending[m] = begin([Stage([joined], [far[m]], list)])[1]
        four, came = end(pending, *markers)
        for m, (a, b) in enumerate(tokens_spans):
            if b == n and a < stages:
                tokens_came[m], arrived = end(tokens_pending[m], *came)
                came = came + arrived
        if n in [b for _, b in spans]:
            feed, _ = end(feed_pending, *came)
    small = four[0][-small.shape[0] :].astype(F32)
    four = jnp.concatenate([four[0][: -small.shape[0]], four[1]])
    _, pending = begin([Stage([four], [move_by(first)], lambda came: came)])
    for m in range(len(far)):
        if m not in tokens_came:
            tokens_came[m], _ = end(tokens_pending[m], *came)
    tokens_grad = run_place(
        after(info, *came), [tokens_own] + [[tokens_came[m][0]] for m in range(len(far))]
    )
    (four_other,), _ = end(pending, tokens_grad)
    four = run_split(mine, four, four_other)
    return (
        mixed,
        tokens_grad,
        four[0],
        small[0],
        four[1],
        four[2],
        small[1],
        four[3],
        small[7],
        up,
        small[9:small_rows].reshape(-1),
        down,
        small[8],
        small[2],
        small[3],
        small[5],
        small[6],
        small[4],
    )


def solution(mesh):
    rows = P("dp", "seq", None)
    in_specs = (rows, P("dp"), rows) + (P(),) * 16
    out_specs = (rows, rows) + (P(),) * 16
    return jax.shard_map(
        on_device, mesh=mesh, in_specs=in_specs, out_specs=out_specs, check_vma=False
    )
```

```python
import functools
import math

import jax
import jax.numpy as jnp
from jax import lax
from jax.experimental import pallas as pl
from jax.experimental.pallas import tpu as pltpu
from jax.sharding import PartitionSpec as P

HEADS = 12
HEAD_DIM = 64
EPSILON = 1e-06
PAIR = 2 * HEAD_DIM
LANES = 128
SCALE = HEAD_DIM ** (-0.5)
SCORE_FACTOR = SCALE * math.log2(math.e)
ROOT_HALF = math.sqrt(0.5)
DENSITY = 1.0 / math.sqrt(2.0 * math.pi)
BELL = -0.5 * math.log2(math.e)
MASKED = -1e30
TILE = 512
MIB = 1024 * 1024
F32 = jnp.float32
BF16 = jnp.bfloat16

QB, VB, OB, G1, S1, G2, S2, RW, DB = range(9)


def cost(microseconds):
    return pl.CostEstimate(
        flops=microseconds * 1_150_000_000, bytes_accessed=1_000_000, transcendentals=0
    )


def nn(a, b):
    return lax.dot_general(a, b, (((1,), (0,)), ((), ())), preferred_element_type=F32)


def nt(a, b):
    return lax.dot_general(a, b, (((1,), (1,)), ((), ())), preferred_element_type=F32)


def tn(a, b):
    return lax.dot_general(a, b, (((0,), (0,)), ((), ())), preferred_element_type=F32)


def hat(field):
    mean = jnp.mean(field, axis=-1, keepdims=True)
    centred = field - mean
    spread = jnp.mean(centred * centred, axis=-1, keepdims=True)
    scale = lax.rsqrt(spread + EPSILON)
    return centred * scale, scale


def hat_back(grad, normal, scale):
    first = jnp.mean(grad, axis=-1, keepdims=True)
    second = jnp.mean(grad * normal, axis=-1, keepdims=True)
    return scale * (grad - first - normal * second)


def row_sum(field):
    return jnp.sum(field, axis=0, keepdims=True)


def head_masks():
    lane = lax.broadcasted_iota(jnp.int32, (1, PAIR), 1)
    return [
        jnp.where(lane < HEAD_DIM, 1.0, 0.0).astype(BF16),
        jnp.where(lane < HEAD_DIM, 0.0, 1.0).astype(BF16),
    ]


def block_at(me, distance, size):
    return pl.ds(pl.multiple_of(jnp.bitwise_xor(me, distance) * size, 16), size)


def attention_kernel(info, *refs, parts):
    came, (vec, wq, wk, wv, wo) = refs[:parts], refs[parts : parts + 5]
    (
        x_ref,
        normed_ref,
        q_ref,
        k_ref,
        v_ref,
        ctx_ref,
        middle_ref,
        one_ref,
        second_ref,
        gate_ref,
        row_ref,
        lse_ref,
    ) = refs[-12:]
    slots = x_ref.shape[1]
    size = slots // parts
    count = info[1 + pl.program_id(0)]
    for distance in range(parts):
        x_ref[0, block_at(info[0], distance, size), :] = came[distance][0]
    x = x_ref[0].astype(F32)
    normal, _ = hat(x)
    normed = (normal * vec[G1 : G1 + 1] + vec[S1 : S1 + 1]).astype(BF16)
    normed_ref[0] = normed
    logit = jnp.sum(normed.astype(F32) * vec[RW : RW + 1], axis=-1, keepdims=True)
    gate = jax.nn.sigmoid(logit)
    inside = lax.broadcasted_iota(jnp.int32, (slots, 1), 0) < count
    row = jnp.where(inside, gate, 0.0)
    gate_ref[0] = jnp.broadcast_to(gate, (slots, LANES))
    row_ref[0] = jnp.broadcast_to(row, (slots, LANES))
    q_ref[0] = (nn(normed, wq[...]) + vec[QB : QB + 1]).astype(BF16)
    k_ref[0] = nn(normed, wk[...]).astype(BF16)
    v_ref[0] = (nn(normed, wv[...]) + vec[VB : VB + 1]).astype(BF16)
    key_mask = jnp.where(
        lax.broadcasted_iota(jnp.int32, (1, slots), 1) < count, 0.0, MASKED
    )
    masks = head_masks()
    lane = lax.broadcasted_iota(jnp.int32, (1, LANES), 1)
    ones = jnp.ones((slots, LANES), BF16)
    lse = jnp.zeros((slots, LANES), F32)
    for pair in range(HEADS // 2):
        at = slice(pair * PAIR, (pair + 1) * PAIR)
        queries = q_ref[0, :, at]
        keys = k_ref[0, :, at]
        values = jnp.concatenate([v_ref[0, :, at], ones], axis=1)
        halves = []
        for e in range(2):
            scores = nt(queries * masks[e], keys) * SCORE_FACTOR + key_mask
            top = jnp.max(scores, axis=-1, keepdims=True)
            expo = jnp.exp2(scores - top).astype(BF16)
            mixed = nn(expo, values)
            total = mixed[:, PAIR:]
            halves.append(mixed[:, :PAIR] / total)
            lse = jnp.where(lane == 2 * pair + e, top + jnp.log2(total), lse)
        low = jnp.where(lane < HEAD_DIM, halves[0], halves[1])
        ctx_ref[0, :, at] = low.astype(BF16)
    lse_ref[0] = lse
    one = nn(ctx_ref[0], wo[...]) + vec[OB : OB + 1]
    one_ref[0] = one.astype(BF16)
    middle = x + row * one
    middle_ref[0] = middle
    again, _ = hat(middle)
    second_ref[0] = (again * vec[G2 : G2 + 1] + vec[S2 : S2 + 1]).astype(BF16)


def run_attention(info, own, came, vectors, weights):
    parts = 1 + len(came)
    images, size, width = came[0].shape
    slots = parts * size
    whole = lambda a: pl.BlockSpec(a.shape, lambda i, c: (0,) * a.ndim)
    outs = [(width, BF16)] * 6 + [(width, F32)] + [(width, BF16)] * 2 + [(LANES, F32)] * 3
    return pl.pallas_call(
        functools.partial(attention_kernel, parts=parts),
        grid_spec=pltpu.PrefetchScalarGridSpec(
            num_scalar_prefetch=1,
            grid=(images,),
            in_specs=[pl.BlockSpec((1, size, width), lambda i, c: (c[0] * images + i, 0, 0))]
            + [pl.BlockSpec((1, size, width), lambda i, c: (i, 0, 0))] * len(came)
            + [whole(a) for a in (vectors, *weights)],
            out_specs=[pl.BlockSpec((1, slots, lanes), lambda i, c: (i, 0, 0)) for lanes, _ in outs],
        ),
        out_shape=[jax.ShapeDtypeStruct((images, slots, lanes), t) for lanes, t in outs],
        compiler_params=pltpu.CompilerParams(vmem_limit_bytes=20 * MIB),
        cost_estimate=cost(20),
        name="attention_forward",
    )(info, own, *came, vectors, *weights)


def feed_kernel(info, second, row, up, bias, down, middle, one, gate, vec, *refs, images):
    parts = (len(refs) - 15) // 2
    came, refs = refs[:parts], refs[parts:]
    mixed, refs = refs[:parts], refs[parts:]
    back_sum, total_ref, low_ref, logit_ref, sums, down_send, down_keep, up_send, up_keep = refs[:9]
    bias_grad, back, flipped, two, pulled, grad_out = refs[9:]
    step = pl.program_id(0)
    size = came[0].shape[1]
    slots = parts * size

    def rows_of(image, distance):
        start = jnp.bitwise_xor(info[0], distance) * size + image * slots
        return pl.ds(pl.multiple_of(start, 16), size)

    @pl.when(step == 0)
    def _():
        total = jnp.zeros(back_sum.shape, F32)
        for image in range(images):
            for distance in range(parts):
                at = rows_of(image, distance)
                upstream = came[distance][image]
                grad_out[at, :] = upstream
                value = (row[at, :1] * upstream.astype(F32)).astype(BF16)
                back[at, :] = value
                total = total + row_sum(value.astype(F32))
        back_sum[...] = total
        flipped[...] = second[...].T
        two[...] = jnp.zeros_like(two)
        pulled[...] = jnp.zeros_like(pulled)

    hidden = nn(second[...], up[...]) + bias[...]
    phi = 0.5 + 0.5 * lax.erf(hidden * ROOT_HALF)
    density = DENSITY * jnp.exp2(hidden * hidden * BELL)
    active = (hidden * phi).astype(BF16)
    slope = phi + hidden * density
    two[...] += nn(active, down[...])
    low = (nt(back[...], down[...]) * slope).astype(BF16)
    bias_grad[...] = row_sum(low.astype(F32))
    pulled[...] += nt(low, up[...])
    down_grad = tn(active, back[...]).astype(BF16)
    up_grad = nn(flipped[...], low).astype(BF16)

    @pl.when(step < pl.num_programs(0) // 2)
    def _():
        down_send[...] = down_grad
        up_send[...] = up_grad

    @pl.when(step >= pl.num_programs(0) // 2)
    def _():
        down_keep[...] = down_grad
        up_keep[...] = up_grad

    @pl.when(step == pl.num_programs(0) - 1)
    def _():
        zero = jnp.zeros((1, second.shape[1]), F32)

        def finish(image, carry):
            gain_sum, shift_sum, one_sum = carry
            for distance in range(parts):
                at = rows_of(image, distance)
                upstream = grad_out[at, :].astype(F32)
                weight = row[at, :1]
                branch_two = two[at, :] + vec[DB : DB + 1]
                centre = middle[at, :]
                mixed[distance][image] = (centre + weight * branch_two).astype(BF16)
                normal, scale = hat(centre)
                grad = pulled[at, :]
                total = hat_back(grad * vec[G2 : G2 + 1], normal, scale) + upstream
                total_ref[at, :] = total.astype(BF16)
                low = (weight * total).astype(BF16)
                low_ref[at, :] = low
                gated = jnp.sum(
                    upstream * branch_two + total * one[at, :].astype(F32), axis=-1, keepdims=True
                )
                logit_ref[at, :] = weight * (1.0 - gate[at, :]) * gated
                gain_sum = gain_sum + row_sum(grad * normal)
                shift_sum = shift_sum + row_sum(grad)
                one_sum = one_sum + row_sum(low.astype(F32))
            return gain_sum, shift_sum, one_sum

        gain_sum, shift_sum, one_sum = lax.fori_loop(0, images, finish, (zero, zero, zero))
        sums[0:1] = gain_sum
        sums[1:2] = shift_sum
        sums[2:3] = one_sum


def shared_out(tiles, step):
    return jnp.minimum(step, tiles - 1), jnp.maximum(step - tiles, 0)


def run_feed(info, second, row, up, bias, down, middle, one, gate, vectors, images, came):
    rows, width = second.shape
    units = up.shape[1]
    tiles = units // TILE // 2
    parts = len(came)
    size = rows // images // parts
    once = dict(pipeline_mode=pl.Buffered(1))
    whole = lambda a, **mode: pl.BlockSpec(a.shape, lambda t, c: (0,) * len(a.shape), **mode)
    tile = lambda t, c: lax.rem(t + (1 - c[1]) * tiles, 2 * tiles)
    shape = jax.ShapeDtypeStruct
    field = lambda dtype: shape((rows, width), dtype)
    outs = [shape((images, size, width), BF16)] * parts
    outs += [shape((1, width), F32), field(BF16), field(BF16), shape(row.shape, F32)]
    outs += [shape((8, width), F32)]
    scratch = [pltpu.VMEM((rows, width), BF16), pltpu.VMEM((width, rows), BF16)]
    scratch += [pltpu.VMEM((rows, width), F32)] * 2 + [pltpu.VMEM((rows, width), BF16)]
    return pl.pallas_call(
        functools.partial(feed_kernel, images=images),
        grid_spec=pltpu.PrefetchScalarGridSpec(
            num_scalar_prefetch=1,
            grid=(2 * tiles,),
            in_specs=[
                whole(second, **once),
                whole(row, **once),
                pl.BlockSpec((width, TILE), lambda t, c: (0, tile(t, c))),
                pl.BlockSpec((1, TILE), lambda t, c: (0, tile(t, c))),
                pl.BlockSpec((TILE, width), lambda t, c: (tile(t, c), 0)),
            ]
            + [whole(a, **once) for a in (middle, one, gate, vectors)]
            + [pl.BlockSpec((images,) + came[0].shape[1:], lambda t, c: (c[0], 0, 0), **once)]
            + [whole(a, **once) for a in came[1:]],
            out_specs=[whole(o, **once) for o in outs]
            + [
                pl.BlockSpec((TILE, width), lambda t, c, n=n: (shared_out(tiles, t)[n], 0))
                for n in range(2)
            ]
            + [
                pl.BlockSpec((width, TILE), lambda t, c, n=n: (0, shared_out(tiles, t)[n]))
                for n in range(2)
            ]
            + [pl.BlockSpec((1, TILE), lambda t, c: (0, tile(t, c)))],
            scratch_shapes=scratch,
        ),
        out_shape=outs
        + [shape((units // 2, width), BF16)] * 2
        + [shape((width, units // 2), BF16)] * 2
        + [shape((1, units), F32)],
        compiler_params=pltpu.CompilerParams(vmem_limit_bytes=34 * MIB),
        cost_estimate=cost(43),
        name="feed",
    )(info, second, row, up, bias, down, middle, one, gate, vectors, *came)


def attention_back_kernel(
    info,
    x_ref,
    q_ref,
    k_ref,
    v_ref,
    lse_ref,
    grad_one,
    grad_middle,
    grad_logit,
    normed,
    vec,
    wq,
    wk,
    wv,
    wo,
    *rest,
    image,
    parts,
):
    grads, *tokens_grad, sums, pulled, tokens_back = rest[-5 - parts + 1 :]
    slots = x_ref.shape[1]
    count = info[1 + image]
    pulled[...] = nt(grad_one[0], wo[...]).astype(BF16)
    lse = lse_ref[0].T
    inside = lax.broadcasted_iota(jnp.int32, (slots, 1), 0) < count
    masks = head_masks()
    for pair in range(HEADS // 2):
        at = slice(pair * PAIR, (pair + 1) * PAIR)
        queries, keys, values = q_ref[0, :, at], k_ref[0, :, at], v_ref[0, :, at]
        above = pulled[:, at]
        grad_q = grad_k = grad_v = None
        for e in range(2):
            h = 2 * pair + e
            own_keys = keys * masks[e]
            scores = nt(own_keys, queries) * SCORE_FACTOR - lse[h : h + 1]
            probs = jnp.exp2(jnp.where(inside, scores, MASKED))
            slope = probs * nt(values * masks[e], above)
            centre = row_sum(slope)
            low = (slope - probs * centre).astype(BF16)
            terms = (
                tn(low, own_keys),
                nn(low, queries * masks[e]),
                nn(probs.astype(BF16), above * masks[e]),
            )
            if e == 0:
                grad_q, grad_k, grad_v = terms
            else:
                grad_q, grad_k, grad_v = (
                    grad_q + terms[0],
                    grad_k + terms[1],
                    grad_v + terms[2],
                )
        grads[0, :, at] = (grad_q * SCALE).astype(BF16)
        grads[1, :, at] = (grad_k * SCALE).astype(BF16)
        grads[2, :, at] = grad_v.astype(BF16)
    logit = grad_logit[0, :, :1]
    total = (
        nt(grads[0], wq[...])
        + nt(grads[1], wk[...])
        + nt(grads[2], wv[...])
        + logit * vec[RW : RW + 1]
    )
    normal, scale = hat(x_ref[0].astype(F32))
    sums[0:1] = row_sum(grads[0].astype(F32))
    sums[1:2] = row_sum(grads[2].astype(F32))
    sums[2:3] = row_sum(total * normal)
    sums[3:4] = row_sum(total)
    sums[4:5] = row_sum(normed[0].astype(F32) * logit)
    back = hat_back(total * vec[G1 : G1 + 1], normal, scale)
    tokens_back[...] = (back + grad_middle[0].astype(F32)).astype(BF16)
    for distance in range(parts):
        tokens_grad[distance][0] = tokens_back[block_at(info[0], distance, slots // parts), :]


def run_attention_back(image, info, fields, vectors, weights, parts):
    images, slots, width = fields[0].shape
    at = lambda a: pl.BlockSpec((1,) + a.shape[1:], lambda i, c: (image, 0, 0))
    whole = lambda a: pl.BlockSpec(a.shape, lambda i, c: (0,) * a.ndim)
    args = [*fields, vectors, *weights]
    in_specs = [at(a) for a in fields] + [whole(a) for a in (vectors, *weights)]
    shape = jax.ShapeDtypeStruct
    size = slots // parts
    return pl.pallas_call(
        functools.partial(attention_back_kernel, image=image, parts=parts),
        grid_spec=pltpu.PrefetchScalarGridSpec(
            num_scalar_prefetch=1,
            grid=(1,),
            in_specs=in_specs,
            out_specs=[pl.BlockSpec((3, slots, width), lambda i, c: (0, 0, 0))]
            + [pl.BlockSpec((1, size, width), lambda i, c: (0, 0, 0))] * parts
            + [pl.BlockSpec((8, width), lambda i, c: (0, 0))],
            scratch_shapes=[pltpu.VMEM((slots, width), BF16)] * 2,
        ),
        out_shape=[shape((3, slots, width), BF16)]
        + [shape((1, size, width), BF16)] * parts
        + [shape((8, width), F32)],
        compiler_params=pltpu.CompilerParams(vmem_limit_bytes=16 * MIB),
        cost_estimate=cost(11),
        name="attention_backward",
    )(info, *args)


def outer_kernel(info, normed, ctx, grad_one, *refs, images):
    grads, (send, keep, flipped, joined) = refs[:images], refs[images:]
    step = pl.program_id(0)
    half = pl.num_programs(0) // 2
    which = lax.rem(step + half * (1 - info[1]), 2 * half)

    @pl.when(step == 0)
    def _():
        flipped[...] = normed[...].T

    @pl.when(which < 3)
    def _():
        slots = grads[0].shape[1]
        for image in range(images):
            joined[image * slots : (image + 1) * slots] = grads[image][0]

    for out, now in ((send, step < half), (keep, step >= half)):

        @pl.when(jnp.logical_and(now, which < 3))
        def _(out=out):
            out[...] = nn(flipped[...], joined[...]).astype(BF16)

        @pl.when(jnp.logical_and(now, which == 3))
        def _(out=out):
            out[...] = tn(ctx[...], grad_one[...]).astype(BF16)


def run_outer(info, normed, ctx, grad_one, grads):
    rows, width = normed.shape
    images = len(grads)
    whole = lambda a: pl.BlockSpec(a.shape, lambda s, c: (0,) * a.ndim)
    return pl.pallas_call(
        functools.partial(outer_kernel, images=images),
        grid_spec=pltpu.PrefetchScalarGridSpec(
            num_scalar_prefetch=1,
            grid=(4,),
            in_specs=[
                whole(normed),
                whole(ctx),
                whole(grad_one),
            ]
            + [
                pl.BlockSpec(
                    (1, rows // images, width),
                    lambda s, c: (jnp.minimum(lax.rem(s + 2 * (1 - c[1]), 4), 2), 0, 0),
                )
            ]
            * images,
            out_specs=[
                pl.BlockSpec((width, width), lambda s, c, n=n: (shared_out(2, s)[n], 0))
                for n in range(2)
            ],
            scratch_shapes=[pltpu.VMEM((width, rows), BF16), pltpu.VMEM((rows, width), BF16)],
        ),
        out_shape=[jax.ShapeDtypeStruct((2 * width, width), BF16)] * 2,
        compiler_params=pltpu.CompilerParams(vmem_limit_bytes=24 * MIB),
        cost_estimate=cost(9),
        name="outer",
    )(info, normed, ctx, grad_one, *grads)


def bits_of(axis):
    size = lax.axis_size(axis)
    count = size.bit_length() - 1
    if size != 1 << count:
        raise ValueError("axis size")
    return [(axis, b) for b in range(count)]


def bit_of(step):
    axis, b = step
    return (lax.axis_index(axis) >> b) & 1


def swap(field, step):
    axis, b = step
    return lax.ppermute(field, axis, [(i, i ^ (1 << b)) for i in range(lax.axis_size(axis))])


def add_low(a, b):
    return (a.astype(F32) + b.astype(F32)).astype(BF16)


def halves(field, step):
    half = field.shape[0] // 2
    own = bit_of(step)
    return (
        lax.dynamic_slice_in_dim(field, (1 - own) * half, half),
        lax.dynamic_slice_in_dim(field, own * half, half),
    )


def ordered(own, other, step, axis=0):
    return jnp.where(
        bit_of(step) == 0,
        jnp.concatenate([own, other], axis=axis),
        jnp.concatenate([other, own], axis=axis),
    )


def spread_kernel(info, own, other, out):
    @pl.when(pl.program_id(0) == 0)
    def _():
        out[...] = own[...].astype(F32)

    @pl.when(pl.program_id(0) == 1)
    def _():
        out[...] = other[...].astype(F32)


def run_spread(info, own, other, axis):
    rows, cols = own.shape
    cuts = 2
    block = (rows // cuts, cols)
    place = lambda h, b: (b, h) if axis else (h * cuts + b, 0)
    still = cuts - 1
    return pl.pallas_call(
        spread_kernel,
        grid_spec=pltpu.PrefetchScalarGridSpec(
            num_scalar_prefetch=1,
            grid=(2, cuts),
            in_specs=[
                pl.BlockSpec(block, lambda h, b, c: (jnp.where(h == 0, b, still), 0)),
                pl.BlockSpec(block, lambda h, b, c: (jnp.where(h == 0, 0, b), 0)),
            ],
            out_specs=pl.BlockSpec(block, lambda h, b, c: place(jnp.bitwise_xor(h, c[1]), b)),
        ),
        out_shape=jax.ShapeDtypeStruct((rows * (2 - axis), cols * (1 + axis)), F32),
        compiler_params=pltpu.CompilerParams(vmem_limit_bytes=20 * MIB),
        cost_estimate=cost(7),
        name="spread",
    )(info, own, other)


def split_kernel(info, own, other, *outs, cuts):
    step = pl.program_id(0)
    for g in range(2):
        for w in range(2):
            start = (jnp.bitwise_xor(g, info[1]) * 2 + w) * cuts
            now = jnp.logical_and(step >= start, step < start + cuts)
            for source, near in ((own, step < 2 * cuts), (other, step >= 2 * cuts)):

                @pl.when(jnp.logical_and(now, near))
                def _(source=source, out=outs[2 * g + w]):
                    out[...] = source[...].astype(F32)


def run_split(info, own, other):
    rows, width = own.shape
    cuts = 1
    side = rows // 2
    block = (side // cuts, width)

    def place(t, c, g, w):
        start = (jnp.bitwise_xor(g, c[1]) * 2 + w) * cuts
        return jnp.clip(t - start, 0, cuts - 1), 0

    return pl.pallas_call(
        functools.partial(split_kernel, cuts=cuts),
        grid_spec=pltpu.PrefetchScalarGridSpec(
            num_scalar_prefetch=1,
            grid=(4 * cuts,),
            in_specs=[
                pl.BlockSpec(block, lambda t, c: (jnp.minimum(t, 2 * cuts - 1), 0)),
                pl.BlockSpec(block, lambda t, c: (jnp.maximum(t - 2 * cuts, 0), 0)),
            ],
            out_specs=[
                pl.BlockSpec(block, functools.partial(place, g=g, w=w))
                for g in range(2)
                for w in range(2)
            ],
        ),
        out_shape=[jax.ShapeDtypeStruct((side, width), F32)] * 4,
        compiler_params=pltpu.CompilerParams(vmem_limit_bytes=24 * MIB),
        cost_estimate=cost(8),
        name="split",
    )(info, own, other)


def swap_far(field, distance):
    size = lax.axis_size("seq")
    return lax.ppermute(field, "seq", [(i, i ^ distance) for i in range(size)])


class Stage:
    def __init__(self, sends, moves, finish):
        self.sends, self.moves, self.finish = sends, moves, finish


def move_by(step):
    return lambda field: swap(field, step)


def move_far(distance):
    return lambda field: swap_far(field, distance)


def scatter_stage(fields, steps):
    pieces = [halves(f, s) for f, s in zip(fields, steps)]
    return Stage(
        [p[0] for p in pieces],
        [move_by(s) for s in steps],
        lambda came: [add_low(p[1], c) for p, c in zip(pieces, came)],
    )


def gather_stage(fields, steps, axis=0):
    return Stage(
        fields,
        [move_by(s) for s in steps],
        lambda came: [ordered(f, c, s, axis) for f, c, s in zip(fields, came, steps)],
    )


def begin(stages, *gates):
    sends = [s for stage in stages for s in stage.sends]
    results = lax.optimization_barrier((*gates, *sends))
    moves = [m for stage in stages for m in stage.moves]
    came = [m(s) for m, s in zip(moves, results[len(gates) :])]
    return list(results[: len(gates)]), (stages, came)


def end(pending, *markers):
    stages, came = pending
    came = list(lax.optimization_barrier((*came, *markers))[: len(came)])
    left, results = came, []
    for stage in stages:
        count = len(stage.sends)
        results.append(stage.finish(left[:count]))
        left = left[count:]
    return (*results, came)


def exchange(*stages):
    return end(begin(stages)[1])[:-1]


def place_kernel(info, *refs, counts):
    *parts, out = refs
    at = 0
    for distance, count in enumerate(counts):

        @pl.when(pl.program_id(0) == distance)
        def _(now=parts[at : at + count]):
            rows = 0
            for part in now:
                out[rows : rows + part.shape[0]] = part[...]
                rows += part.shape[0]

        at += count


def run_place(info, parts):
    size, width = parts[0][0].shape[1:]
    images = sum(p.shape[0] for p in parts[0])
    args = [p for group in parts for p in group]
    return pl.pallas_call(
        functools.partial(place_kernel, counts=[len(group) for group in parts]),
        grid_spec=pltpu.PrefetchScalarGridSpec(
            num_scalar_prefetch=1,
            grid=(len(parts),),
            in_specs=[pl.BlockSpec(a.shape, lambda d, c: (0, 0, 0)) for a in args],
            out_specs=pl.BlockSpec(
                (images, size, width), lambda d, c: (jnp.bitwise_xor(c[0], d), 0, 0)
            ),
        ),
        out_shape=jax.ShapeDtypeStruct((len(parts) * images, size, width), BF16),
        compiler_params=pltpu.CompilerParams(vmem_limit_bytes=16 * MIB),
        cost_estimate=cost(3),
        name="place",
    )(info, *args)


def after(value, *others):
    return lax.optimization_barrier((value, *others))[0]


def on_device(
    tokens,
    lengths,
    grad_out,
    query_weight,
    query_bias,
    key_weight,
    value_weight,
    value_bias,
    output_weight,
    output_bias,
    up_weight,
    up_bias,
    down_weight,
    down_bias,
    first_gain,
    first_shift,
    second_gain,
    second_shift,
    router_weight,
):
    parts = lax.axis_size("seq")
    me = lax.axis_index("seq").astype(jnp.int32)
    group, size, width = tokens.shape
    images = group // parts
    slots = parts * size
    rows = images * slots
    distances = range(1, parts)
    blocks_for = lambda field, d: lax.dynamic_slice_in_dim(field, (me ^ d) * images, images)
    came = [swap_far(blocks_for(tokens, d), d) for d in distances]
    grad_came = [grad_out]
    for d in distances:
        grad_came.append(swap_far(after(blocks_for(grad_out, d), came[-1]), d))

    lengths = lax.dynamic_slice_in_dim(lengths, me * images, images)
    info = jnp.concatenate([me.reshape(1), (lengths + 1) // 2])
    vectors = [
        query_bias,
        value_bias,
        output_bias,
        first_gain,
        first_shift,
        second_gain,
        second_shift,
        router_weight,
        down_bias,
    ]
    vectors = jnp.pad(jnp.stack(vectors).astype(F32), ((0, 16 - len(vectors)), (0, 0)))
    flat = lambda field: field.reshape(rows, field.shape[-1])
    cube = lambda field: field.reshape(images, slots, field.shape[-1])

    weights = (query_weight, key_weight, value_weight, output_weight)
    x, normed, queries, keys, values, context, middle, one, second, gate, row, lse = run_attention(
        info, tokens, came, vectors, weights
    )

    first, *others = bits_of("dp")
    crossed = others[::-1]
    own = bit_of(first)
    mine = jnp.stack([me, own])
    far = [move_far(d) for d in distances]

    seq_bits = bits_of("seq")
    pair = lambda n: (others[n], crossed[n])
    core = lambda sent, kept: Stage([sent], [move_by(first)], lambda came: [add_low(kept, came[0])])
    join = lambda fields: [jnp.concatenate(fields)]

    *mixed, back_sum, grad_middle, grad_one, grad_logit, sums, down_send, down_keep, up_send, up_keep, bias_grad = (
        run_feed(
            after(mine, *grad_came[1:]),
            flat(second),
            flat(row),
            up_weight,
            up_bias[None].astype(F32),
            down_weight,
            flat(middle),
            flat(one),
            flat(gate),
            vectors,
            images,
            grad_came,
        )
    )
    (gated,), pending = begin(
        [Stage([down_send, up_send], [move_by(first)] * 2, lambda came: came)], info
    )
    feed_came, came = end(pending)
    feed = [add_low(down_keep, feed_came[0]), add_low(up_keep, feed_came[1])]
    (gated,), pending = begin([scatter_stage(feed, pair(0))], after(gated, *came))
    mixed_came = [
        begin([Stage([after(part, gated)], [move], list)])[1] for part, move in zip(mixed[1:], far)
    ]

    fields = (
        x,
        queries,
        keys,
        values,
        lse,
        cube(grad_one),
        cube(grad_middle),
        cube(grad_logit),
        normed,
    )
    tokens_parts = []
    left = [("xy", n) for n in range(1, len(others))] + [("z", s) for s in seq_bits]

    def feed_stage(feed):
        kind, step = left.pop(0)
        if kind == "xy":
            return scatter_stage(feed, pair(step))
        if len(feed) == 2:
            feed = [jnp.concatenate([feed[0], feed[1].reshape(-1, width)])]
        return scatter_stage(feed, [step])

    grads = []
    for image in range(images):
        image_grads, *part, image_sums = run_attention_back(
            image, gated, fields, vectors, weights, parts
        )
        grads.append(image_grads)
        tokens_parts.append(part)
        small = small + image_sums if image else image_sums
        extra = []
        if image < len(mixed_came):
            (mixed_came[image],), extra = end(mixed_came[image], image_sums)
            gated = after(gated, *extra)
        if image == images - 2 or images == 1:
            feed, came = end(pending, image_sums)
            while len(left) > 3:
                (feed,) = exchange(feed_stage(feed))
            (gated,), pending = begin([feed_stage(feed)], after(gated, *came))
    feed, came = end(pending, image_sums)
    joined = lambda m: jnp.concatenate([part[m] for part in tokens_parts])
    tokens_own = [part[0] for part in tokens_parts]
    tokens_came = {0: None}
    near = Stage([joined(1)], far[:1], list)
    (gated,), pending = begin([feed_stage(feed), near], after(mine, *came, *extra))
    four_send, four_keep = run_outer(gated, flat(normed), flat(context), grad_one, grads)
    feed, tokens_came[0], came = end(pending, four_keep[:8])
    mixed_left = images

    small = jnp.concatenate(
        [
            small[:5],
            sums[:3],
            back_sum,
            bias_grad.reshape(-1, width),
        ]
    )
    small_rows = small.shape[0]
    cut = 1 << (len(others) + len(seq_bits))
    small = jnp.pad(small, ((0, -small_rows % cut), (0, 0)))

    def four_parts(came):
        total = add_low(four_keep, came[0])
        half = total.shape[0] // 2
        return [
            jnp.concatenate([total[:half], (small + came[1]).astype(BF16)]),
            total[half:],
        ]

    def feed_back_stage(step, feed):
        kind, step = step
        if kind == "last":
            return feed_stage(feed)
        if kind == "z":
            return gather_stage(feed, [step])
        if len(feed) == 1:
            half = feed[0].shape[0] // 2
            feed = [feed[0][:half], feed[0][half:].reshape(-1, up_keep.shape[1])]
        if kind == "xy":
            return gather_stage(feed, pair(step))
        return Stage(feed, [move_by(first)] * 2, lambda came: list(zip(feed, came)))

    feed_left = [("last", None)] * len(left) + [("z", s) for s in reversed(seq_bits)]
    feed_left += [("xy", n) for n in reversed(range(len(others)))] + [("core", first)]
    four_left = [("core", first)] + [("cut", n) for n in range(len(others))]
    four_left += [("join", s) for s in seq_bits] + [("bind", s) for s in reversed(seq_bits)]
    four_left += [("grow", n) for n in reversed(range(len(others)))]
    count = len(feed_left)
    spans = [(0, 0), (1, 1), (2, 2), (3, 4), (5, 6), (7, 7)]
    if count != len(spans):
        spans = [(n, n) for n in range(count)]
    stages = len(four_left)
    four, feed_pending, widths, came = None, None, None, None
    tokens_spans = [(-1, -1), (5, 6), (3, 4)][: len(far)]
    tokens_spans += [(0, stages)] * (len(far) - len(tokens_spans))
    tokens_pending = {}
    for n, (kind, step) in enumerate(four_left):
        if kind == "core":
            stage = Stage([four_send, small], [move_by(first)] * 2, four_parts)
        elif kind == "cut":
            stage = scatter_stage(four, pair(step))
        elif kind == "join":
            if len(four) == 2:
                widths = four[0].shape[0]
                four = join(four)
            stage = scatter_stage(four, [step])
        elif kind == "bind":
            stage = gather_stage(four, [step])
        else:
            if len(four) == 1:
                four = [four[0][:widths], four[0][widths:]]
            stage = gather_stage(four, pair(step))
        starts = [a for a, _ in spans]
        if n in starts:
            more = feed_back_stage(feed_left[starts.index(n)], feed)
            _, (_, moving) = begin([stage, more])
            count = len(stage.sends)
            pending, feed_pending = ([stage], moving[:count]), ([more], moving[count:])
        else:
            _, pending = begin([stage])
        markers = []
        if n == 1:
            for m in range(mixed_left, len(mixed_came)):
                (mixed_came[m],), _ = end(mixed_came[m])
            mixed = run_place(after(info, *came), [[mixed[0]]] + [[c] for c in mixed_came])
            markers = [mixed]
        if n == stages - 1:
            down, up = (
                run_spread(after(mine, *came), *pair_of, axis) for axis, pair_of in enumerate(feed)
            )
            markers = [down, up]
        for m, (a, b) in enumerate(tokens_spans):
            if a == n and m not in tokens_pending:
                sent = joined(m + 1) if came is None else after(joined(m + 1), *came)
                tokens_pending[m] = begin([Stage([sent], [far[m]], list)])[1]
        four, came = end(pending, *markers)
        for m, (a, b) in enumerate(tokens_spans):
            if b == n:
                tokens_came[m], arrived = end(tokens_pending[m], *came)
                came = came + arrived
        if n in [b for _, b in spans]:
            feed, _ = end(feed_pending, *came)
    small = four[0][-small.shape[0] :].astype(F32)
    four = jnp.concatenate([four[0][: -small.shape[0]], four[1]])
    _, pending = begin([Stage([four], [move_by(first)], lambda came: came)])
    for m in range(len(far)):
        if m not in tokens_came:
            tokens_came[m], _ = end(tokens_pending[m], *came)
    tokens_grad = run_place(
        after(info, *came), [tokens_own] + [[tokens_came[m][0]] for m in range(len(far))]
    )
    (four_other,), _ = end(pending, tokens_grad)
    four = run_split(mine, four, four_other)
    return (
        mixed,
        tokens_grad,
        four[0],
        small[0],
        four[1],
        four[2],
        small[1],
        four[3],
        small[7],
        up,
        small[9:small_rows].reshape(-1),
        down,
        small[8],
        small[2],
        small[3],
        small[5],
        small[6],
        small[4],
    )


def solution(mesh):
    rows = P("dp", "seq", None)
    in_specs = (rows, P("dp"), rows) + (P(),) * 16
    out_specs = (rows, rows) + (P(),) * 16
    return jax.shard_map(
        on_device, mesh=mesh, in_specs=in_specs, out_specs=out_specs, check_vma=False
    )
```

```python
import functools
import math

import jax
import jax.numpy as jnp
from jax import lax
from jax.experimental import pallas as pl
from jax.experimental.pallas import tpu as pltpu
from jax.sharding import PartitionSpec as P

HEADS = 12
HEAD_DIM = 64
EPSILON = 1e-06
PAIR = 2 * HEAD_DIM
LANES = 128
SCALE = HEAD_DIM ** (-0.5)
SCORE_FACTOR = SCALE * math.log2(math.e)
ROOT_HALF = math.sqrt(0.5)
DENSITY = 1.0 / math.sqrt(2.0 * math.pi)
BELL = -0.5 * math.log2(math.e)
MASKED = -1e30
TILE = 512
MIB = 1024 * 1024
F32 = jnp.float32
BF16 = jnp.bfloat16

QB, VB, OB, G1, S1, G2, S2, RW, DB = range(9)


def cost(microseconds):
    return pl.CostEstimate(
        flops=microseconds * 1_150_000_000, bytes_accessed=1_000_000, transcendentals=0
    )


def nn(a, b):
    return lax.dot_general(a, b, (((1,), (0,)), ((), ())), preferred_element_type=F32)


def nt(a, b):
    return lax.dot_general(a, b, (((1,), (1,)), ((), ())), preferred_element_type=F32)


def tn(a, b):
    return lax.dot_general(a, b, (((0,), (0,)), ((), ())), preferred_element_type=F32)


def hat(field):
    mean = jnp.mean(field, axis=-1, keepdims=True)
    centred = field - mean
    spread = jnp.mean(centred * centred, axis=-1, keepdims=True)
    scale = lax.rsqrt(spread + EPSILON)
    return centred * scale, scale


def hat_back(grad, normal, scale):
    first = jnp.mean(grad, axis=-1, keepdims=True)
    second = jnp.mean(grad * normal, axis=-1, keepdims=True)
    return scale * (grad - first - normal * second)


def row_sum(field):
    return jnp.sum(field, axis=0, keepdims=True)


def head_masks():
    lane = lax.broadcasted_iota(jnp.int32, (1, PAIR), 1)
    return [
        jnp.where(lane < HEAD_DIM, 1.0, 0.0).astype(BF16),
        jnp.where(lane < HEAD_DIM, 0.0, 1.0).astype(BF16),
    ]


def block_at(me, distance, size):
    return pl.ds(pl.multiple_of(jnp.bitwise_xor(me, distance) * size, 16), size)


def attention_kernel(info, *refs, parts):
    came, (vec, wq, wk, wv, wo) = refs[:parts], refs[parts : parts + 5]
    (
        x_ref,
        normed_ref,
        q_ref,
        k_ref,
        v_ref,
        ctx_ref,
        middle_ref,
        one_ref,
        second_ref,
        gate_ref,
        row_ref,
        lse_ref,
    ) = refs[-12:]
    slots = x_ref.shape[1]
    size = slots // parts
    count = info[1 + pl.program_id(0)]
    for distance in range(parts):
        x_ref[0, block_at(info[0], distance, size), :] = came[distance][0]
    x = x_ref[0].astype(F32)
    normal, _ = hat(x)
    normed = (normal * vec[G1 : G1 + 1] + vec[S1 : S1 + 1]).astype(BF16)
    normed_ref[0] = normed
    logit = jnp.sum(normed.astype(F32) * vec[RW : RW + 1], axis=-1, keepdims=True)
    gate = jax.nn.sigmoid(logit)
    inside = lax.broadcasted_iota(jnp.int32, (slots, 1), 0) < count
    row = jnp.where(inside, gate, 0.0)
    gate_ref[0] = jnp.broadcast_to(gate, (slots, LANES))
    row_ref[0] = jnp.broadcast_to(row, (slots, LANES))
    q_ref[0] = (nn(normed, wq[...]) + vec[QB : QB + 1]).astype(BF16)
    k_ref[0] = nn(normed, wk[...]).astype(BF16)
    v_ref[0] = (nn(normed, wv[...]) + vec[VB : VB + 1]).astype(BF16)
    key_mask = jnp.where(
        lax.broadcasted_iota(jnp.int32, (1, slots), 1) < count, 0.0, MASKED
    )
    masks = head_masks()
    lane = lax.broadcasted_iota(jnp.int32, (1, LANES), 1)
    ones = jnp.ones((slots, LANES), BF16)
    lse = jnp.zeros((slots, LANES), F32)
    for pair in range(HEADS // 2):
        at = slice(pair * PAIR, (pair + 1) * PAIR)
        queries = q_ref[0, :, at]
        keys = k_ref[0, :, at]
        values = jnp.concatenate([v_ref[0, :, at], ones], axis=1)
        halves = []
        for e in range(2):
            scores = nt(queries * masks[e], keys) * SCORE_FACTOR + key_mask
            top = jnp.max(scores, axis=-1, keepdims=True)
            expo = jnp.exp2(scores - top).astype(BF16)
            mixed = nn(expo, values)
            total = mixed[:, PAIR:]
            halves.append(mixed[:, :PAIR] / total)
            lse = jnp.where(lane == 2 * pair + e, top + jnp.log2(total), lse)
        low = jnp.where(lane < HEAD_DIM, halves[0], halves[1])
        ctx_ref[0, :, at] = low.astype(BF16)
    lse_ref[0] = lse
    one = nn(ctx_ref[0], wo[...]) + vec[OB : OB + 1]
    one_ref[0] = one.astype(BF16)
    middle = x + row * one
    middle_ref[0] = middle
    again, _ = hat(middle)
    second_ref[0] = (again * vec[G2 : G2 + 1] + vec[S2 : S2 + 1]).astype(BF16)


def run_attention(info, own, came, vectors, weights):
    parts = 1 + len(came)
    images, size, width = came[0].shape
    slots = parts * size
    whole = lambda a: pl.BlockSpec(a.shape, lambda i, c: (0,) * a.ndim)
    outs = [(width, BF16)] * 6 + [(width, F32)] + [(width, BF16)] * 2 + [(LANES, F32)] * 3
    return pl.pallas_call(
        functools.partial(attention_kernel, parts=parts),
        grid_spec=pltpu.PrefetchScalarGridSpec(
            num_scalar_prefetch=1,
            grid=(images,),
            in_specs=[pl.BlockSpec((1, size, width), lambda i, c: (c[0] * images + i, 0, 0))]
            + [pl.BlockSpec((1, size, width), lambda i, c: (i, 0, 0))] * len(came)
            + [whole(a) for a in (vectors, *weights)],
            out_specs=[pl.BlockSpec((1, slots, lanes), lambda i, c: (i, 0, 0)) for lanes, _ in outs],
        ),
        out_shape=[jax.ShapeDtypeStruct((images, slots, lanes), t) for lanes, t in outs],
        compiler_params=pltpu.CompilerParams(vmem_limit_bytes=20 * MIB),
        cost_estimate=cost(20),
        name="attention_forward",
    )(info, own, *came, vectors, *weights)


def feed_kernel(info, second, row, up, bias, down, middle, one, gate, vec, *refs, images):
    parts = (len(refs) - 15) // 2
    came, refs = refs[:parts], refs[parts:]
    mixed, refs = refs[:parts], refs[parts:]
    back_sum, total_ref, low_ref, logit_ref, sums, down_send, down_keep, up_send, up_keep = refs[:9]
    bias_grad, back, flipped, two, pulled, grad_out = refs[9:]
    step = pl.program_id(0)
    size = came[0].shape[1]
    slots = parts * size

    def rows_of(image, distance):
        start = jnp.bitwise_xor(info[0], distance) * size + image * slots
        return pl.ds(pl.multiple_of(start, 16), size)

    @pl.when(step == 0)
    def _():
        total = jnp.zeros(back_sum.shape, F32)
        for image in range(images):
            for distance in range(parts):
                at = rows_of(image, distance)
                upstream = came[distance][image]
                grad_out[at, :] = upstream
                value = (row[at, :1] * upstream.astype(F32)).astype(BF16)
                back[at, :] = value
                total = total + row_sum(value.astype(F32))
        back_sum[...] = total
        flipped[...] = second[...].T
        two[...] = jnp.zeros_like(two)
        pulled[...] = jnp.zeros_like(pulled)

    hidden = nn(second[...], up[...]) + bias[...]
    phi = 0.5 + 0.5 * lax.erf(hidden * ROOT_HALF)
    density = DENSITY * jnp.exp2(hidden * hidden * BELL)
    active = (hidden * phi).astype(BF16)
    slope = phi + hidden * density
    two[...] += nn(active, down[...])
    low = (nt(back[...], down[...]) * slope).astype(BF16)
    bias_grad[...] = row_sum(low.astype(F32))
    pulled[...] += nt(low, up[...])
    down_grad = tn(active, back[...]).astype(BF16)
    up_grad = nn(flipped[...], low).astype(BF16)

    @pl.when(step < pl.num_programs(0) // 2)
    def _():
        down_send[...] = down_grad
        up_send[...] = up_grad

    @pl.when(step >= pl.num_programs(0) // 2)
    def _():
        down_keep[...] = down_grad
        up_keep[...] = up_grad

    @pl.when(step == pl.num_programs(0) - 1)
    def _():
        zero = jnp.zeros((1, second.shape[1]), F32)

        def finish(image, carry):
            gain_sum, shift_sum, one_sum = carry
            for distance in range(parts):
                at = rows_of(image, distance)
                upstream = grad_out[at, :].astype(F32)
                weight = row[at, :1]
                branch_two = two[at, :] + vec[DB : DB + 1]
                centre = middle[at, :]
                mixed[distance][image] = (centre + weight * branch_two).astype(BF16)
                normal, scale = hat(centre)
                grad = pulled[at, :]
                total = hat_back(grad * vec[G2 : G2 + 1], normal, scale) + upstream
                total_ref[at, :] = total.astype(BF16)
                low = (weight * total).astype(BF16)
                low_ref[at, :] = low
                gated = jnp.sum(
                    upstream * branch_two + total * one[at, :].astype(F32), axis=-1, keepdims=True
                )
                logit_ref[at, :] = weight * (1.0 - gate[at, :]) * gated
                gain_sum = gain_sum + row_sum(grad * normal)
                shift_sum = shift_sum + row_sum(grad)
                one_sum = one_sum + row_sum(low.astype(F32))
            return gain_sum, shift_sum, one_sum

        gain_sum, shift_sum, one_sum = lax.fori_loop(0, images, finish, (zero, zero, zero))
        sums[0:1] = gain_sum
        sums[1:2] = shift_sum
        sums[2:3] = one_sum


def shared_out(tiles, step):
    return jnp.minimum(step, tiles - 1), jnp.maximum(step - tiles, 0)


def run_feed(info, second, row, up, bias, down, middle, one, gate, vectors, images, came):
    rows, width = second.shape
    units = up.shape[1]
    tiles = units // TILE // 2
    parts = len(came)
    size = rows // images // parts
    once = dict(pipeline_mode=pl.Buffered(1))
    whole = lambda a, **mode: pl.BlockSpec(a.shape, lambda t, c: (0,) * len(a.shape), **mode)
    tile = lambda t, c: lax.rem(t + (1 - c[1]) * tiles, 2 * tiles)
    shape = jax.ShapeDtypeStruct
    field = lambda dtype: shape((rows, width), dtype)
    outs = [shape((images, size, width), BF16)] * parts
    outs += [shape((1, width), F32), field(BF16), field(BF16), shape(row.shape, F32)]
    outs += [shape((8, width), F32)]
    scratch = [pltpu.VMEM((rows, width), BF16), pltpu.VMEM((width, rows), BF16)]
    scratch += [pltpu.VMEM((rows, width), F32)] * 2 + [pltpu.VMEM((rows, width), BF16)]
    return pl.pallas_call(
        functools.partial(feed_kernel, images=images),
        grid_spec=pltpu.PrefetchScalarGridSpec(
            num_scalar_prefetch=1,
            grid=(2 * tiles,),
            in_specs=[
                whole(second, **once),
                whole(row, **once),
                pl.BlockSpec((width, TILE), lambda t, c: (0, tile(t, c))),
                pl.BlockSpec((1, TILE), lambda t, c: (0, tile(t, c))),
                pl.BlockSpec((TILE, width), lambda t, c: (tile(t, c), 0)),
            ]
            + [whole(a, **once) for a in (middle, one, gate, vectors)]
            + [pl.BlockSpec((images,) + came[0].shape[1:], lambda t, c: (c[0], 0, 0), **once)]
            + [whole(a, **once) for a in came[1:]],
            out_specs=[whole(o, **once) for o in outs]
            + [
                pl.BlockSpec((TILE, width), lambda t, c, n=n: (shared_out(tiles, t)[n], 0))
                for n in range(2)
            ]
            + [
                pl.BlockSpec((width, TILE), lambda t, c, n=n: (0, shared_out(tiles, t)[n]))
                for n in range(2)
            ]
            + [pl.BlockSpec((1, TILE), lambda t, c: (0, tile(t, c)))],
            scratch_shapes=scratch,
        ),
        out_shape=outs
        + [shape((units // 2, width), BF16)] * 2
        + [shape((width, units // 2), BF16)] * 2
        + [shape((1, units), F32)],
        compiler_params=pltpu.CompilerParams(vmem_limit_bytes=34 * MIB),
        cost_estimate=cost(43),
        name="feed",
    )(info, second, row, up, bias, down, middle, one, gate, vectors, *came)


def attention_back_kernel(
    info,
    x_ref,
    q_ref,
    k_ref,
    v_ref,
    lse_ref,
    grad_one,
    grad_middle,
    grad_logit,
    normed,
    vec,
    wq,
    wk,
    wv,
    wo,
    *rest,
    image,
    parts,
):
    grads, *tokens_grad, sums, pulled, tokens_back = rest[-5 - parts + 1 :]
    slots = x_ref.shape[1]
    count = info[1 + image]
    pulled[...] = nt(grad_one[0], wo[...]).astype(BF16)
    lse = lse_ref[0].T
    inside = lax.broadcasted_iota(jnp.int32, (slots, 1), 0) < count
    masks = head_masks()
    for pair in range(HEADS // 2):
        at = slice(pair * PAIR, (pair + 1) * PAIR)
        queries, keys, values = q_ref[0, :, at], k_ref[0, :, at], v_ref[0, :, at]
        above = pulled[:, at]
        grad_q = grad_k = grad_v = None
        for e in range(2):
            h = 2 * pair + e
            own_keys = keys * masks[e]
            scores = nt(own_keys, queries) * SCORE_FACTOR - lse[h : h + 1]
            probs = jnp.exp2(jnp.where(inside, scores, MASKED))
            slope = probs * nt(values * masks[e], above)
            centre = row_sum(slope)
            low = (slope - probs * centre).astype(BF16)
            terms = (
                tn(low, own_keys),
                nn(low, queries * masks[e]),
                nn(probs.astype(BF16), above * masks[e]),
            )
            if e == 0:
                grad_q, grad_k, grad_v = terms
            else:
                grad_q, grad_k, grad_v = (
                    grad_q + terms[0],
                    grad_k + terms[1],
                    grad_v + terms[2],
                )
        grads[0, :, at] = (grad_q * SCALE).astype(BF16)
        grads[1, :, at] = (grad_k * SCALE).astype(BF16)
        grads[2, :, at] = grad_v.astype(BF16)
    logit = grad_logit[0, :, :1]
    total = (
        nt(grads[0], wq[...])
        + nt(grads[1], wk[...])
        + nt(grads[2], wv[...])
        + logit * vec[RW : RW + 1]
    )
    normal, scale = hat(x_ref[0].astype(F32))
    sums[0:1] = row_sum(grads[0].astype(F32))
    sums[1:2] = row_sum(grads[2].astype(F32))
    sums[2:3] = row_sum(total * normal)
    sums[3:4] = row_sum(total)
    sums[4:5] = row_sum(normed[0].astype(F32) * logit)
    back = hat_back(total * vec[G1 : G1 + 1], normal, scale)
    tokens_back[...] = (back + grad_middle[0].astype(F32)).astype(BF16)
    for distance in range(parts):
        tokens_grad[distance][0] = tokens_back[block_at(info[0], distance, slots // parts), :]


def run_attention_back(image, info, fields, vectors, weights, parts):
    images, slots, width = fields[0].shape
    at = lambda a: pl.BlockSpec((1,) + a.shape[1:], lambda i, c: (image, 0, 0))
    whole = lambda a: pl.BlockSpec(a.shape, lambda i, c: (0,) * a.ndim)
    args = [*fields, vectors, *weights]
    in_specs = [at(a) for a in fields] + [whole(a) for a in (vectors, *weights)]
    shape = jax.ShapeDtypeStruct
    size = slots // parts
    return pl.pallas_call(
        functools.partial(attention_back_kernel, image=image, parts=parts),
        grid_spec=pltpu.PrefetchScalarGridSpec(
            num_scalar_prefetch=1,
            grid=(1,),
            in_specs=in_specs,
            out_specs=[pl.BlockSpec((3, slots, width), lambda i, c: (0, 0, 0))]
            + [pl.BlockSpec((1, size, width), lambda i, c: (0, 0, 0))] * parts
            + [pl.BlockSpec((8, width), lambda i, c: (0, 0))],
            scratch_shapes=[pltpu.VMEM((slots, width), BF16)] * 2,
        ),
        out_shape=[shape((3, slots, width), BF16)]
        + [shape((1, size, width), BF16)] * parts
        + [shape((8, width), F32)],
        compiler_params=pltpu.CompilerParams(vmem_limit_bytes=16 * MIB),
        cost_estimate=cost(11),
        name="attention_backward",
    )(info, *args)


def outer_kernel(info, normed, ctx, grad_one, *refs, images):
    grads, (send, keep, flipped, joined) = refs[:images], refs[images:]
    step = pl.program_id(0)
    half = pl.num_programs(0) // 2
    which = lax.rem(step + half * (1 - info[1]), 2 * half)

    @pl.when(step == 0)
    def _():
        flipped[...] = normed[...].T

    @pl.when(which < 3)
    def _():
        slots = grads[0].shape[1]
        for image in range(images):
            joined[image * slots : (image + 1) * slots] = grads[image][0]

    for out, now in ((send, step < half), (keep, step >= half)):

        @pl.when(jnp.logical_and(now, which < 3))
        def _(out=out):
            out[...] = nn(flipped[...], joined[...]).astype(BF16)

        @pl.when(jnp.logical_and(now, which == 3))
        def _(out=out):
            out[...] = tn(ctx[...], grad_one[...]).astype(BF16)


def run_outer(info, normed, ctx, grad_one, grads):
    rows, width = normed.shape
    images = len(grads)
    whole = lambda a: pl.BlockSpec(a.shape, lambda s, c: (0,) * a.ndim)
    return pl.pallas_call(
        functools.partial(outer_kernel, images=images),
        grid_spec=pltpu.PrefetchScalarGridSpec(
            num_scalar_prefetch=1,
            grid=(4,),
            in_specs=[
                whole(normed),
                whole(ctx),
                whole(grad_one),
            ]
            + [
                pl.BlockSpec(
                    (1, rows // images, width),
                    lambda s, c: (jnp.minimum(lax.rem(s + 2 * (1 - c[1]), 4), 2), 0, 0),
                )
            ]
            * images,
            out_specs=[
                pl.BlockSpec((width, width), lambda s, c, n=n: (shared_out(2, s)[n], 0))
                for n in range(2)
            ],
            scratch_shapes=[pltpu.VMEM((width, rows), BF16), pltpu.VMEM((rows, width), BF16)],
        ),
        out_shape=[jax.ShapeDtypeStruct((2 * width, width), BF16)] * 2,
        compiler_params=pltpu.CompilerParams(vmem_limit_bytes=24 * MIB),
        cost_estimate=cost(9),
        name="outer",
    )(info, normed, ctx, grad_one, *grads)


def bits_of(axis):
    size = lax.axis_size(axis)
    count = size.bit_length() - 1
    if size != 1 << count:
        raise ValueError("axis size")
    return [(axis, b) for b in range(count)]


def bit_of(step):
    axis, b = step
    return (lax.axis_index(axis) >> b) & 1


def swap(field, step):
    axis, b = step
    return lax.ppermute(field, axis, [(i, i ^ (1 << b)) for i in range(lax.axis_size(axis))])


def add_low(a, b):
    return (a.astype(F32) + b.astype(F32)).astype(BF16)


def halves(field, step):
    half = field.shape[0] // 2
    own = bit_of(step)
    return (
        lax.dynamic_slice_in_dim(field, (1 - own) * half, half),
        lax.dynamic_slice_in_dim(field, own * half, half),
    )


def ordered(own, other, step, axis=0):
    return jnp.where(
        bit_of(step) == 0,
        jnp.concatenate([own, other], axis=axis),
        jnp.concatenate([other, own], axis=axis),
    )


def spread_kernel(info, own, other, out):
    @pl.when(pl.program_id(0) == 0)
    def _():
        out[...] = own[...].astype(F32)

    @pl.when(pl.program_id(0) == 1)
    def _():
        out[...] = other[...].astype(F32)


def run_spread(info, own, other, axis):
    rows, cols = own.shape
    cuts = 2
    block = (rows // cuts, cols)
    place = lambda h, b: (b, h) if axis else (h * cuts + b, 0)
    still = cuts - 1
    return pl.pallas_call(
        spread_kernel,
        grid_spec=pltpu.PrefetchScalarGridSpec(
            num_scalar_prefetch=1,
            grid=(2, cuts),
            in_specs=[
                pl.BlockSpec(block, lambda h, b, c: (jnp.where(h == 0, b, still), 0)),
                pl.BlockSpec(block, lambda h, b, c: (jnp.where(h == 0, 0, b), 0)),
            ],
            out_specs=pl.BlockSpec(block, lambda h, b, c: place(jnp.bitwise_xor(h, c[1]), b)),
        ),
        out_shape=jax.ShapeDtypeStruct((rows * (2 - axis), cols * (1 + axis)), F32),
        compiler_params=pltpu.CompilerParams(vmem_limit_bytes=20 * MIB),
        cost_estimate=cost(7),
        name="spread",
    )(info, own, other)


def split_kernel(info, own, other, *outs, cuts):
    step = pl.program_id(0)
    for g in range(2):
        for w in range(2):
            start = (jnp.bitwise_xor(g, info[1]) * 2 + w) * cuts
            now = jnp.logical_and(step >= start, step < start + cuts)
            for source, near in ((own, step < 2 * cuts), (other, step >= 2 * cuts)):

                @pl.when(jnp.logical_and(now, near))
                def _(source=source, out=outs[2 * g + w]):
                    out[...] = source[...].astype(F32)


def run_split(info, own, other):
    rows, width = own.shape
    cuts = 1
    side = rows // 2
    block = (side // cuts, width)

    def place(t, c, g, w):
        start = (jnp.bitwise_xor(g, c[1]) * 2 + w) * cuts
        return jnp.clip(t - start, 0, cuts - 1), 0

    return pl.pallas_call(
        functools.partial(split_kernel, cuts=cuts),
        grid_spec=pltpu.PrefetchScalarGridSpec(
            num_scalar_prefetch=1,
            grid=(4 * cuts,),
            in_specs=[
                pl.BlockSpec(block, lambda t, c: (jnp.minimum(t, 2 * cuts - 1), 0)),
                pl.BlockSpec(block, lambda t, c: (jnp.maximum(t - 2 * cuts, 0), 0)),
            ],
            out_specs=[
                pl.BlockSpec(block, functools.partial(place, g=g, w=w))
                for g in range(2)
                for w in range(2)
            ],
        ),
        out_shape=[jax.ShapeDtypeStruct((side, width), F32)] * 4,
        compiler_params=pltpu.CompilerParams(vmem_limit_bytes=24 * MIB),
        cost_estimate=cost(8),
        name="split",
    )(info, own, other)


def swap_far(field, distance):
    size = lax.axis_size("seq")
    return lax.ppermute(field, "seq", [(i, i ^ distance) for i in range(size)])


class Stage:
    def __init__(self, sends, moves, finish):
        self.sends, self.moves, self.finish = sends, moves, finish


def move_by(step):
    return lambda field: swap(field, step)


def move_far(distance):
    return lambda field: swap_far(field, distance)


def scatter_stage(fields, steps):
    pieces = [halves(f, s) for f, s in zip(fields, steps)]
    return Stage(
        [p[0] for p in pieces],
        [move_by(s) for s in steps],
        lambda came: [add_low(p[1], c) for p, c in zip(pieces, came)],
    )


def gather_stage(fields, steps, axis=0):
    return Stage(
        fields,
        [move_by(s) for s in steps],
        lambda came: [ordered(f, c, s, axis) for f, c, s in zip(fields, came, steps)],
    )


def begin(stages, *gates):
    sends = [s for stage in stages for s in stage.sends]
    results = lax.optimization_barrier((*gates, *sends))
    moves = [m for stage in stages for m in stage.moves]
    came = [m(s) for m, s in zip(moves, results[len(gates) :])]
    return list(results[: len(gates)]), (stages, came)


def end(pending, *markers):
    stages, came = pending
    came = list(lax.optimization_barrier((*came, *markers))[: len(came)])
    left, results = came, []
    for stage in stages:
        count = len(stage.sends)
        results.append(stage.finish(left[:count]))
        left = left[count:]
    return (*results, came)


def exchange(*stages):
    return end(begin(stages)[1])[:-1]


def place_kernel(info, *refs, counts):
    *parts, out = refs
    at = 0
    for distance, count in enumerate(counts):

        @pl.when(pl.program_id(0) == distance)
        def _(now=parts[at : at + count]):
            rows = 0
            for part in now:
                out[rows : rows + part.shape[0]] = part[...]
                rows += part.shape[0]

        at += count


def run_place(info, parts):
    size, width = parts[0][0].shape[1:]
    images = sum(p.shape[0] for p in parts[0])
    args = [p for group in parts for p in group]
    return pl.pallas_call(
        functools.partial(place_kernel, counts=[len(group) for group in parts]),
        grid_spec=pltpu.PrefetchScalarGridSpec(
            num_scalar_prefetch=1,
            grid=(len(parts),),
            in_specs=[pl.BlockSpec(a.shape, lambda d, c: (0, 0, 0)) for a in args],
            out_specs=pl.BlockSpec(
                (images, size, width), lambda d, c: (jnp.bitwise_xor(c[0], d), 0, 0)
            ),
        ),
        out_shape=jax.ShapeDtypeStruct((len(parts) * images, size, width), BF16),
        compiler_params=pltpu.CompilerParams(vmem_limit_bytes=16 * MIB),
        cost_estimate=cost(3),
        name="place",
    )(info, *args)


def after(value, *others):
    return lax.optimization_barrier((value, *others))[0]


def on_device(
    tokens,
    lengths,
    grad_out,
    query_weight,
    query_bias,
    key_weight,
    value_weight,
    value_bias,
    output_weight,
    output_bias,
    up_weight,
    up_bias,
    down_weight,
    down_bias,
    first_gain,
    first_shift,
    second_gain,
    second_shift,
    router_weight,
):
    parts = lax.axis_size("seq")
    me = lax.axis_index("seq").astype(jnp.int32)
    group, size, width = tokens.shape
    images = group // parts
    slots = parts * size
    rows = images * slots
    distances = range(1, parts)
    blocks_for = lambda field, d: lax.dynamic_slice_in_dim(field, (me ^ d) * images, images)
    came = [swap_far(blocks_for(tokens, d), d) for d in distances]
    grad_came = [grad_out]
    for d in distances:
        grad_came.append(swap_far(after(blocks_for(grad_out, d), came[-1]), d))

    lengths = lax.dynamic_slice_in_dim(lengths, me * images, images)
    info = jnp.concatenate([me.reshape(1), (lengths + 1) // 2])
    vectors = [
        query_bias,
        value_bias,
        output_bias,
        first_gain,
        first_shift,
        second_gain,
        second_shift,
        router_weight,
        down_bias,
    ]
    vectors = jnp.pad(jnp.stack(vectors).astype(F32), ((0, 16 - len(vectors)), (0, 0)))
    flat = lambda field: field.reshape(rows, field.shape[-1])
    cube = lambda field: field.reshape(images, slots, field.shape[-1])

    weights = (query_weight, key_weight, value_weight, output_weight)
    x, normed, queries, keys, values, context, middle, one, second, gate, row, lse = run_attention(
        info, tokens, came, vectors, weights
    )

    first, *others = bits_of("dp")
    crossed = others[::-1]
    own = bit_of(first)
    mine = jnp.stack([me, own])
    far = [move_far(d) for d in distances]

    seq_bits = bits_of("seq")
    pair = lambda n: (others[n], crossed[n])
    core = lambda sent, kept: Stage([sent], [move_by(first)], lambda came: [add_low(kept, came[0])])
    join = lambda fields: [jnp.concatenate(fields)]

    *mixed, back_sum, grad_middle, grad_one, grad_logit, sums, down_send, down_keep, up_send, up_keep, bias_grad = (
        run_feed(
            after(mine, *grad_came[1:]),
            flat(second),
            flat(row),
            up_weight,
            up_bias[None].astype(F32),
            down_weight,
            flat(middle),
            flat(one),
            flat(gate),
            vectors,
            images,
            grad_came,
        )
    )
    (gated,), pending = begin(
        [Stage([down_send, up_send], [move_by(first)] * 2, lambda came: came)], info
    )
    feed_came, came = end(pending)
    feed = [add_low(down_keep, feed_came[0]), add_low(up_keep, feed_came[1])]
    (gated,), pending = begin([scatter_stage(feed, pair(0))], after(gated, *came))
    send_back = lambda m, *gates: begin([Stage([after(mixed[m + 1], *gates)], [far[m]], list)])[1]
    mixed_came = {len(far) - 1: send_back(len(far) - 1, gated)}

    fields = (
        x,
        queries,
        keys,
        values,
        lse,
        cube(grad_one),
        cube(grad_middle),
        cube(grad_logit),
        normed,
    )
    tokens_parts = []
    left = [("xy", n) for n in range(1, len(others))] + [("z", s) for s in seq_bits]

    def feed_stage(feed):
        kind, step = left.pop(0)
        if kind == "xy":
            return scatter_stage(feed, pair(step))
        if len(feed) == 2:
            feed = [jnp.concatenate([feed[0], feed[1].reshape(-1, width)])]
        return scatter_stage(feed, [step])

    grads = []
    for image in range(images):
        image_grads, *part, image_sums = run_attention_back(
            image, gated, fields, vectors, weights, parts
        )
        grads.append(image_grads)
        tokens_parts.append(part)
        small = small + image_sums if image else image_sums
        extra = []
        if image == 0:
            for m in range(len(far) - 1):
                mixed_came[m] = send_back(m, image_sums)
        turn = len(far) - image
        if image and turn in mixed_came:
            (mixed_came[turn],), extra = end(mixed_came[turn], image_sums)
            gated = after(gated, *extra)
        if image == images - 2 or images == 1:
            feed, came = end(pending, image_sums)
            while len(left) > 3:
                (feed,) = exchange(feed_stage(feed))
            (gated,), pending = begin([feed_stage(feed)], after(gated, *came))
    feed, came = end(pending, image_sums)
    joined = lambda m: jnp.concatenate([part[m] for part in tokens_parts])
    tokens_own = [part[0] for part in tokens_parts]
    tokens_came = {0: None}
    near = Stage([joined(1)], far[:1], list)
    (gated,), pending = begin([feed_stage(feed), near], after(mine, *came, *extra))
    four_send, four_keep = run_outer(gated, flat(normed), flat(context), grad_one, grads)
    feed, tokens_came[0], came = end(pending, four_keep[:8])
    mixed_left = images

    small = jnp.concatenate(
        [
            small[:5],
            sums[:3],
            back_sum,
            bias_grad.reshape(-1, width),
        ]
    )
    small_rows = small.shape[0]
    cut = 1 << (len(others) + len(seq_bits))
    small = jnp.pad(small, ((0, -small_rows % cut), (0, 0)))

    def four_parts(came):
        total = add_low(four_keep, came[0])
        half = total.shape[0] // 2
        return [
            jnp.concatenate([total[:half], (small + came[1]).astype(BF16)]),
            total[half:],
        ]

    def feed_back_stage(step, feed):
        kind, step = step
        if kind == "last":
            return feed_stage(feed)
        if kind == "z":
            return gather_stage(feed, [step])
        if len(feed) == 1:
            half = feed[0].shape[0] // 2
            feed = [feed[0][:half], feed[0][half:].reshape(-1, up_keep.shape[1])]
        if kind == "xy":
            return gather_stage(feed, pair(step))
        return Stage(feed, [move_by(first)] * 2, lambda came: list(zip(feed, came)))

    feed_left = [("last", None)] * len(left) + [("z", s) for s in reversed(seq_bits)]
    feed_left += [("xy", n) for n in reversed(range(len(others)))] + [("core", first)]
    four_left = [("core", first)] + [("cut", n) for n in range(len(others))]
    four_left += [("join", s) for s in seq_bits] + [("bind", s) for s in reversed(seq_bits)]
    four_left += [("grow", n) for n in reversed(range(len(others)))]
    count = len(feed_left)
    spans = [(0, 0), (1, 1), (2, 2), (3, 4), (5, 6), (7, 7)]
    if count != len(spans):
        spans = [(n, n) for n in range(count)]
    stages = len(four_left)
    four, feed_pending, widths, came = None, None, None, None
    tokens_spans = [(-1, -1), (5, 6), (3, 4)][: len(far)]
    tokens_spans += [(0, stages)] * (len(far) - len(tokens_spans))
    tokens_pending = {}
    for n, (kind, step) in enumerate(four_left):
        if kind == "core":
            stage = Stage([four_send, small], [move_by(first)] * 2, four_parts)
        elif kind == "cut":
            stage = scatter_stage(four, pair(step))
        elif kind == "join":
            if len(four) == 2:
                widths = four[0].shape[0]
                four = join(four)
            stage = scatter_stage(four, [step])
        elif kind == "bind":
            stage = gather_stage(four, [step])
        else:
            if len(four) == 1:
                four = [four[0][:widths], four[0][widths:]]
            stage = gather_stage(four, pair(step))
        starts = [a for a, _ in spans]
        if n in starts:
            more = feed_back_stage(feed_left[starts.index(n)], feed)
            _, (_, moving) = begin([stage, more])
            count = len(stage.sends)
            pending, feed_pending = ([stage], moving[:count]), ([more], moving[count:])
        else:
            _, pending = begin([stage])
        markers = []
        if n == 1:
            for m in range(len(far) - images + 1):
                (mixed_came[m],), _ = end(mixed_came[m])
            mixed = run_place(after(info, *came), [[mixed[0]]] + [[mixed_came[m]] for m in range(len(far))])
            markers = [mixed]
        if n == stages - 1:
            down, up = (
                run_spread(after(mine, *came), *pair_of, axis) for axis, pair_of in enumerate(feed)
            )
            markers = [down, up]
        for m, (a, b) in enumerate(tokens_spans):
            if a == n and m not in tokens_pending:
                sent = joined(m + 1) if came is None else after(joined(m + 1), *came)
                tokens_pending[m] = begin([Stage([sent], [far[m]], list)])[1]
        four, came = end(pending, *markers)
        for m, (a, b) in enumerate(tokens_spans):
            if b == n:
                tokens_came[m], arrived = end(tokens_pending[m], *came)
                came = came + arrived
        if n in [b for _, b in spans]:
            feed, _ = end(feed_pending, *came)
    small = four[0][-small.shape[0] :].astype(F32)
    four = jnp.concatenate([four[0][: -small.shape[0]], four[1]])
    _, pending = begin([Stage([four], [move_by(first)], lambda came: came)])
    for m in range(len(far)):
        if m not in tokens_came:
            tokens_came[m], _ = end(tokens_pending[m], *came)
    tokens_grad = run_place(
        after(info, *came), [tokens_own] + [[tokens_came[m][0]] for m in range(len(far))]
    )
    (four_other,), _ = end(pending, tokens_grad)
    four = run_split(mine, four, four_other)
    return (
        mixed,
        tokens_grad,
        four[0],
        small[0],
        four[1],
        four[2],
        small[1],
        four[3],
        small[7],
        up,
        small[9:small_rows].reshape(-1),
        down,
        small[8],
        small[2],
        small[3],
        small[5],
        small[6],
        small[4],
    )


def solution(mesh):
    rows = P("dp", "seq", None)
    in_specs = (rows, P("dp"), rows) + (P(),) * 16
    out_specs = (rows, rows) + (P(),) * 16
    return jax.shard_map(
        on_device, mesh=mesh, in_specs=in_specs, out_specs=out_specs, check_vma=False
    )
```
